512 devices in a mesh: stream: 16 (over z), vert: 8 (over y, core), span: 4 (over x).
Axes of the slice: x: 4, y: 4, z: 16, core: 2. Of those that a mesh axis runs over, the one named last changes fastest.
Arguments:
- forcing: float32 [128, 128, 512], P('stream', 'vert', 'span'), may hold values from -6 to 6
- geometry: float32 [4, 16, 16, 64], P(None, 'stream', 'vert', 'span'), may hold values from 0.02 to 0.2
- wall_elem: int32 [512, 64], P(('stream', 'vert', 'span')), may hold values from 0 to 31
- wall_face: int32 [512, 64], P(('stream', 'vert', 'span')), may hold values from 0 to 5
- wall_store: int32 [512, 64], P(('stream', 'vert', 'span')), may hold values from 0 to 4, as said below
- wall_weight: float32 [512, 4096], P(('stream', 'vert', 'span')), may hold values from 0.00034526698 to 0.0013810679
- wall_arm: float32 [512, 3, 4096], P(('stream', 'vert', 'span')), may hold values from -6 to 6
- store_motion: float32 [6, 4], replicated, may hold values from -6 to 6
- store_inverse: float32 [4, 4], replicated, may hold values from 1 to 4
Outputs:
- pressure: float32 [128, 128, 512], P('stream', 'vert', 'span')
- mesh_velocity: float32 [512, 3, 4096], P(('stream', 'vert', 'span'))
The draws below stay inside these ranges and needn't reach their ends.
Inputs may be any that keep to these rules, and one draw needn't show every extreme that they name: `wall_store`: on each device the live slots come first; some device has all 64 slots live and some has none.
All inputs are finite; a program needn't handle non-finite values.
Results may differ from the reference program's by a relative error of at most 0.0003.
Values sent between devices are 32-bit elements; how exact they have to be, the bound alone decides.
No kernel may reach another device: no remote copies, remote signals or barrier semaphores. Data moves between devices by JAX's collectives and lax.ppermute only.
A program may use at most 64 MiB of HBM per device.

```python
import math
import jax
import jax.numpy as jnp
import numpy as np
from jax import lax

EX = 1
EY = 2
EZ = 16
ITERS = 2
STORES = 4
WALL_CAP = 64
STREAM_ELEMENTS = 16
VERTICAL_ELEMS = 16
SPAN_ELEMENTS = 64
DEVICE_COUNT = 512
WALL_ROWS = 4096
N_VERT = 8
N_SPAN = 4


def draw_wall_store(key, part):
    key = jax.random.fold_in(key, 7)
    first, second, third = jax.random.split(key, 3)
    raw = jax.random.randint(first, (DEVICE_COUNT,), 0, WALL_CAP + 1)
    counts = raw * raw // WALL_CAP
    fullest = jax.random.randint(third, (), 0, DEVICE_COUNT)
    emptiest = (fullest + 1) % DEVICE_COUNT
    ranks = jnp.arange(DEVICE_COUNT)
    counts = jnp.where(ranks == fullest, WALL_CAP, counts)
    counts = jnp.where(ranks == emptiest, 0, counts)
    stores = jax.random.randint(second, (DEVICE_COUNT, WALL_CAP), 0, STORES)
    slots = jnp.arange(WALL_CAP)[None, :]
    return jnp.where(slots < counts[:, None], stores, STORES).astype(jnp.int32)


def touch_ends(values, stream_key, smallest, high):
    longest = values.shape.index(max(values.shape))
    spots = []
    for shift in (0, 1):
        where = [jax.random.randint(jax.random.fold_in(stream_key, axis), (), 0, length) for axis, length in enumerate(values.shape)]
        where[longest] = (where[longest] + shift) % values.shape[longest]
        spots.append(tuple(where))
    return values.at[spots[0]].set(smallest).at[spots[1]].set(high)


def block_levels(stream_key, dims, pieces, low, largest):
    factor_of = 1.0
    for dim, parts in pieces:
        heights = jax.random.uniform(jax.random.fold_in(jax.random.fold_in(stream_key, 6), dim), (parts,), jnp.float32, low / len(pieces), largest / len(pieces))
        factor_of = factor_of * jnp.repeat(jnp.exp(heights), dims[dim] // parts).reshape((-1,) + (1,) * (len(dims) - 1 - dim))
    return factor_of


def normal_values(own_key, extent, width, bound, cuts=(), kind=jnp.bfloat16):
    drawn = width * jax.random.normal(own_key, extent, jnp.float32)
    if cuts:
        drawn = drawn * block_levels(own_key, extent, cuts, -0.22, 0.18)
    return jnp.clip(drawn, -bound, bound).astype(kind)


def setup_inputs(seed: int = 0) -> dict:
    arg_keys = jax.random.split(jax.random.key(seed), 10)
    forcing = normal_values(arg_keys[0], (STREAM_ELEMENTS * 8, VERTICAL_ELEMS * 8, SPAN_ELEMENTS * 8), 1.0, 6.0, ((0, 16), (1, 8), (2, 4)), jnp.float32)
    geometry = jnp.clip(jnp.exp(math.log(0.2) - 2.3025851 * jax.random.uniform(arg_keys[1], (4, STREAM_ELEMENTS, VERTICAL_ELEMS, SPAN_ELEMENTS), jnp.float32) ** block_levels(arg_keys[1], (4, STREAM_ELEMENTS, VERTICAL_ELEMS, SPAN_ELEMENTS), ((1, 16), (2, 8), (3, 4)), -0.2, 0.2)), 0.02, 0.2)
    wall_elem = touch_ends(jax.random.randint(arg_keys[2], (DEVICE_COUNT, WALL_CAP), 0, EX * EY * EZ), jax.random.fold_in(arg_keys[2], 1), 0, (EX * EY * EZ) - 1).astype(jnp.int32)
    wall_face = touch_ends(jax.random.randint(arg_keys[3], (DEVICE_COUNT, WALL_CAP), 0, 6), jax.random.fold_in(arg_keys[3], 1), 0, 5).astype(jnp.int32)
    wall_store = draw_wall_store(jax.random.fold_in(arg_keys[9], 71), 0)
    wall_weight = jnp.clip(jnp.exp(math.log(0.0013810679) - 1.3862944 * jax.random.uniform(arg_keys[5], (DEVICE_COUNT, WALL_ROWS), jnp.float32) ** block_levels(arg_keys[5], (DEVICE_COUNT, WALL_ROWS), ((0, 512),), -0.2, 0.2)), 0.00034526698, 0.0013810679)
    wall_arm = normal_values(arg_keys[6], (DEVICE_COUNT, 3, WALL_ROWS), 1.0, 6.0, ((0, 512),), jnp.float32)
    store_motion = normal_values(arg_keys[7], (6, STORES), 1.0, 6.0, (), jnp.float32)
    store_inverse = jnp.clip(jnp.exp(jax.random.uniform(arg_keys[8], (4, STORES), jnp.float32, math.log(1.0), math.log(4.0))), 1.0, 4.0)
    return {"forcing": forcing, "geometry": geometry, "wall_elem": wall_elem, "wall_face": wall_face, "wall_store": wall_store, "wall_weight": wall_weight, "wall_arm": wall_arm, "store_motion": store_motion, "store_inverse": store_inverse}


precise = lax.Precision.HIGHEST
gll_inner = [-0.8717401485096066, -0.5917001814331423, -0.2092992179024789, 0.2092992179024789, 0.5917001814331423, 0.8717401485096066]


def legendre_seven(points):
    before = points * 0.0 + 1.0
    current = points * 1.0
    for order in range(1, 7):
        following = ((2 * order + 1) * points * current - order * before) / (order + 1)
        before = current
        current = following
    return current


def gll_tables():
    degree = 7
    points = np.array([-1.0] + gll_inner + [1.0])
    legendre_at = legendre_seven(points)
    weights = 2.0 / (degree * (degree + 1) * legendre_at ** 2)
    derivative = np.zeros((8, 8))
    for i in range(8):
        for j in range(8):
            if i != j:
                derivative[i, j] = legendre_at[i] / (legendre_at[j] * (points[i] - points[j]))
    derivative[0, 0] = -degree * (degree + 1) / 4.0
    derivative[7, 7] = degree * (degree + 1) / 4.0
    return jnp.asarray(derivative, dtype=jnp.float32), jnp.asarray(weights, dtype=jnp.float32)


def apply_local(field, geometry, derivative, weights):
    ex, ey, ez = geometry.shape[1], geometry.shape[2], geometry.shape[3]
    blocks = field.reshape(ex, 8, ey, 8, ez, 8)
    cube = weights[:, None, None] * weights[None, :, None] * weights[None, None, :]
    cube = cube[None, :, None, :, None, :]

    def scaled(node_values, factor):
        return node_values * (factor[:, None, :, None, :, None] * cube)

    grad_a = jnp.einsum("pi,aibjck->apbjck", derivative, blocks, precision=precise)
    grad_b = jnp.einsum("pj,aibjck->aibpck", derivative, blocks, precision=precise)
    grad_c = jnp.einsum("pk,aibjck->aibjcp", derivative, blocks, precision=precise)
    total = jnp.einsum("pi,apbjck->aibjck", derivative, scaled(grad_a, geometry[0]), precision=precise)
    total = total + jnp.einsum("pj,aibpck->aibjck", derivative, scaled(grad_b, geometry[1]), precision=precise)
    total = total + jnp.einsum("pk,aibjcp->aibjck", derivative, scaled(grad_c, geometry[2]), precision=precise)
    total = total + scaled(blocks, 50.0 * geometry[3])
    return total.reshape(field.shape)


def add_along(padded, axis):
    size = padded.shape[axis] - 2
    before = lax.slice_in_dim(padded, 0, size, axis=axis)
    centre = lax.slice_in_dim(padded, 1, size + 1, axis=axis)
    after = lax.slice_in_dim(padded, 2, size + 2, axis=axis)
    position = lax.broadcasted_iota(jnp.int32, centre.shape, axis) % 8
    return centre + jnp.where(position == 0, before, 0.0) + jnp.where(position == 7, after, 0.0)


def assemble(field):
    for axis in range(3):
        element_widths = [(1, 1) if other == axis else (0, 0) for other in range(3)]
        field = add_along(jnp.pad(field, element_widths), axis)
    return field


def apply_global(field, geometry, derivative, weights):
    slabs = field.reshape(geometry.shape[1], 8, field.shape[1], field.shape[2])
    geo_slabs = jnp.transpose(geometry, (1, 0, 2, 3))[:, :, None, :, :]

    def apply_slab_operator(items):
        return apply_local(items[0], items[1], derivative, weights)

    return lax.map(apply_slab_operator, (slabs, geo_slabs)).reshape(field.shape)


def face_values(field, elems, faces, start_x, start_y, start_z, ey, ez):
    def one_block(elem):
        corner_x = ((start_x + elem // (ey * ez)) * 8).astype(jnp.int32)
        vertical_corner = ((start_y + (elem // ez) % ey) * 8).astype(jnp.int32)
        spanwise_corner = ((start_z + elem % ez) * 8).astype(jnp.int32)
        return lax.dynamic_slice(field, (corner_x, vertical_corner, spanwise_corner), (8, 8, 8))

    blocks = jax.vmap(one_block)(elems)
    count = elems.shape[0]
    sides = jnp.stack([blocks[:, 0], blocks[:, 7], blocks[:, :, 0], blocks[:, :, 7], blocks[:, :, :, 0], blocks[:, :, :, 7]], axis=1)
    sides = sides.reshape(count, 6, 64)
    pick = (jnp.arange(6, dtype=jnp.int32)[None, :] == faces[:, None]).astype(field.dtype)
    return jnp.sum(sides * pick[:, :, None], axis=1).reshape(count * 64)


def cross(left, right):
    return jnp.stack([left[1] * right[2] - left[2] * right[1], left[2] * right[0] - left[0] * right[2], left[0] * right[1] - left[1] * right[0]])


def store_onehot(stores, count_stores, dtype):
    store_rows = jnp.repeat(stores, 64)
    return (jnp.arange(count_stores, dtype=jnp.int32)[:, None] == store_rows[None, :]).astype(dtype)


def wall_loads(node_values, faces, stores, weights, arms, count_stores):
    face_rows = jnp.repeat(faces, 64)
    sign = (2 * (face_rows % 2) - 1).astype(node_values.dtype)
    direction = face_rows // 2
    push = -node_values * weights * sign
    traction = jnp.stack([jnp.where(direction == comp, push, 0.0) for comp in range(3)])
    loads = jnp.concatenate([traction, cross(arms, traction)], axis=0)
    onehot = store_onehot(stores, count_stores, node_values.dtype)
    return jnp.einsum("lr,sr->ls", loads, onehot, precision=precise)


def rigid_motion(totals, motion, inverse, stores, arms):
    onehot = store_onehot(stores, motion.shape[1], totals.dtype)
    linear = motion[0:3] + inverse[0:1] * totals[0:3]
    angular = motion[3:6] + inverse[1:4] * totals[3:6]
    linear_rows = jnp.einsum("cs,sr->cr", linear, onehot, precision=precise)
    angular_rows = jnp.einsum("cs,sr->cr", angular, onehot, precision=precise)
    return linear_rows + cross(angular_rows, arms)


def reference(forcing, geometry, wall_elem, wall_face, wall_store, wall_weight, wall_arm, store_motion, store_inverse):
    derivative, weights = gll_tables()
    inverse_mult = 1.0 / assemble(jnp.ones_like(forcing))
    right = assemble(forcing)
    pressure = jnp.zeros_like(forcing)
    residual = right
    direction = right
    norm_now = jnp.sum(residual * residual * inverse_mult)
    for step in range(ITERS):
        image = assemble(apply_global(direction, geometry, derivative, weights))
        alpha = norm_now / jnp.sum(direction * image * inverse_mult)
        pressure = pressure + alpha * direction
        residual = residual - alpha * image
        if step + 1 < ITERS:
            norm_next = jnp.sum(residual * residual * inverse_mult)
            direction = residual + (norm_next / norm_now) * direction
            norm_now = norm_next

    def device_partial(device, elems, faces, stores, weights_row, arms):
        start_x = device // (N_VERT * N_SPAN) * EX
        start_y = (device // N_SPAN) % N_VERT * EY
        start_z = device % N_SPAN * EZ
        node_values = face_values(pressure, elems, faces, start_x, start_y, start_z, EY, EZ)
        return wall_loads(node_values, faces, stores, weights_row, arms, STORES)

    devices = jnp.arange(DEVICE_COUNT, dtype=jnp.int32)
    partials = jax.vmap(device_partial)(devices, wall_elem, wall_face, wall_store, wall_weight, wall_arm)
    totals = jnp.sum(partials, axis=0)

    def device_velocity(stores, arms):
        return rigid_motion(totals, store_motion, store_inverse, stores, arms)

    mesh_velocity = jax.vmap(device_velocity)(wall_store, wall_arm)
    return pressure, mesh_velocity
```

```python
import functools

import jax
import jax.numpy as jnp
import numpy as np
from jax import lax
from jax.experimental import pallas as pl
from jax.experimental.pallas import tpu as pltpu
from jax.sharding import PartitionSpec as P

F32 = jnp.float32
AXES = ("stream", "vert", "span")
SHARDS = P(AXES, None)
gll_inner = [
    -0.8717401485096066,
    -0.5917001814331423,
    -0.2092992179024789,
    0.2092992179024789,
    0.5917001814331423,
    0.8717401485096066,
]
MOMENTS = (((1, 2, 1.0), (2, 1, -1.0)), ((0, 2, -1.0), (2, 0, 1.0)), ((0, 1, 1.0), (1, 0, -1.0)))


def legendre_seven(points):
    before = points * 0.0 + 1.0
    current = points * 1.0
    for order in range(1, 7):
        following = ((2 * order + 1) * points * current - order * before) / (order + 1)
        before = current
        current = following
    return current


def gll_tables():
    degree = 7
    points = np.array([-1.0] + gll_inner + [1.0])
    legendre_at = legendre_seven(points)
    weights = 2.0 / (degree * (degree + 1) * legendre_at**2)
    derivative = np.zeros((8, 8))
    for i in range(8):
        for j in range(8):
            if i != j:
                derivative[i, j] = legendre_at[i] / (legendre_at[j] * (points[i] - points[j]))
    derivative[0, 0] = -degree * (degree + 1) / 4.0
    derivative[7, 7] = degree * (degree + 1) / 4.0
    return derivative, weights


DERIV, WEIGHTS = gll_tables()
STIFF = DERIV.T @ np.diag(WEIGHTS) @ DERIV


def constants():
    def f32(a):
        return np.asarray(a, np.float32)

    lane_k = f32(np.kron(np.eye(16), STIFF))
    lane_i = f32(np.kron(np.eye(2), np.kron(STIFF, np.eye(8))))
    rows = f32(np.kron(np.eye(32), STIFF))
    wj = np.tile(WEIGHTS[:, None], (1, 128))
    wk = np.tile(np.tile(WEIGHTS, 16)[None], (8, 1))
    wi = np.tile(np.tile(np.repeat(WEIGHTS, 8), 2)[None], (8, 1))
    return lane_k, lane_i, rows, f32(np.concatenate([wj, wk, wi], axis=0))


def dot(a, b):
    return lax.dot_general(
        a,
        b,
        (((1,), (0,)), ((), ())),
        precision=lax.Precision.HIGHEST,
        preferred_element_type=F32,
    )


def lane_sums(rows):
    return lax.dot_general(
        jnp.ones((8, 128), F32),
        rows,
        (((1,), (1,)), ((), ())),
        precision=lax.Precision.HIGHEST,
        preferred_element_type=F32,
    )


def row_ids():
    return lax.broadcasted_iota(jnp.int32, (8, 128), 0)


def lane_ids(rows=8):
    return lax.broadcasted_iota(jnp.int32, (rows, 128), 1)


def join_rows(below, above):
    row = row_ids()
    new_below = below + jnp.where(row == 7, pltpu.roll(above, 7, 0), 0.0)
    new_above = above + jnp.where(row == 0, pltpu.roll(below, 1, 0), 0.0)
    return new_below, new_above


def join_lanes(tile):
    lane = lane_ids()
    k = lane % 8
    left = jnp.where((k == 0) & (lane > 0), pltpu.roll(tile, 1, 1), 0.0)
    right = jnp.where((k == 7) & (lane < 127), pltpu.roll(tile, 127, 1), 0.0)
    return tile + left + right


def call(body, outs, cost=2000, **kwargs):
    vmem = pl.BlockSpec(memory_space=pltpu.VMEM)

    def run(*args, smem=0):
        specs = [pl.BlockSpec(memory_space=pltpu.SMEM)] * smem + [vmem] * (len(args) - smem)
        return pl.pallas_call(
            body,
            out_shape=[jax.ShapeDtypeStruct(s, F32) for s in outs],
            in_specs=specs,
            out_specs=[vmem] * len(outs),
            compiler_params=pltpu.CompilerParams(vmem_limit_bytes=16 * 2**20),
            cost_estimate=pl.CostEstimate(flops=cost * 1000, bytes_accessed=200000, transcendentals=0),
            **kwargs,
        )(*args)

    return run


def stream_added(f_ref, low_ref, high_ref, geo_ref, x_ref, up_ref, down_ref):
    for i in range(8):
        a = f_ref[i, 0:8, :]
        b = f_ref[i, 8:16, :]
        if i == 0:
            a = a + low_ref[0:8, :]
            b = b + low_ref[8:16, :]
        if i == 7:
            a = a + high_ref[0:8, :]
            b = b + high_ref[8:16, :]
        a, b = join_rows(a, b)
        x_ref[i, 0:8, :] = a
        x_ref[i, 8:16, :] = b
        down_ref[8 * i : 8 * i + 8, :] = a
        up_ref[8 * i : 8 * i + 8, :] = b
    down_ref[64:72, :] = geo_ref[...]
    up_ref[64:72, :] = geo_ref[...]


def vert_added(x_ref, low_ref, high_ref, geo_ref, v_ref, g_ref, right_ref, left_ref):
    v = lax.axis_index("vert")
    has_low = jnp.where(v > 0, 1.0, 0.0)
    has_high = jnp.where(v < 7, 1.0, 0.0)
    lane = lane_ids()
    right = [jnp.zeros((8, 128), F32) for _ in range(4)]
    left = [jnp.zeros((8, 128), F32) for _ in range(4)]
    for i in range(8):
        rows = slice(8 * i, 8 * i + 8)
        low, a = join_rows(low_ref[rows, :] * has_low, x_ref[i, 0:8, :])
        b, high = join_rows(x_ref[i, 8:16, :], high_ref[rows, :] * has_high)
        for t, tile in enumerate((low, a, b, high)):
            tile = join_lanes(tile)
            v_ref[i, 8 * t : 8 * t + 8, :] = tile
            to_right = pltpu.roll(tile, (8 * i - 120) % 128, 1)
            to_left = pltpu.roll(tile, 64 + 8 * i, 1)
            right[t] = jnp.where(lane // 8 == i, to_right, right[t])
            left[t] = jnp.where(lane // 8 == 8 + i, to_left, left[t])
    for t in range(4):
        right_ref[8 * t : 8 * t + 8, :] = right[t]
        left_ref[8 * t : 8 * t + 8, :] = left[t]
    geo = geo_ref[...]
    geo_low = low_ref[64:72, :] * has_low
    geo_high = high_ref[64:72, :] * has_high
    rows = []
    for d in range(4):
        rows.append(geo_low[2 * d + 1 : 2 * d + 2, :])
        rows.append(geo[2 * d : 2 * d + 2, :])
        rows.append(geo_high[2 * d : 2 * d + 1, :])
    extended = jnp.concatenate(rows, axis=0)
    g_ref[...] = extended
    wide = lane_ids(16)
    last = jnp.broadcast_to(extended[:, 127:128], (16, 128))
    first = jnp.broadcast_to(extended[:, 0:1], (16, 128))
    right_ref[32:48, :] = jnp.where(wide < 64, last, 0.0)
    left_ref[32:48, :] = jnp.where(wide >= 64, first, 0.0)


def node_rows(geo, d, t):
    return jnp.broadcast_to(geo[4 * d + t : 4 * d + t + 1, :], (8, 128))


def span_added(
    v_ref, g_ref, right_ref, left_ref, low_ref, high_ref, kk_ref, ki_ref, kr_ref, w_ref,
    v0_ref, local_ref, part_ref, top_ref, bottom_ref, maps_ref, field,
):
    lane = lane_ids()
    wj, wk, wi = w_ref[0:8, :], w_ref[8:16, :], w_ref[16:24, :]
    got = [low_ref[8 * t : 8 * t + 8, :] + high_ref[8 * t : 8 * t + 8, :] for t in range(4)]
    halo = []
    for t in range(4):
        rows = slice(8 * t, 8 * t + 8)
        from_own_first = pltpu.roll(left_ref[rows, :], 71, 1)
        from_own_last = pltpu.roll(right_ref[rows, :], 57, 1)
        tile = got[t] + jnp.where((lane < 64) & (lane % 8 == 7), from_own_first, 0.0)
        halo.append(tile + jnp.where((lane >= 64) & (lane % 8 == 0), from_own_last, 0.0))
    own = [[None] * 4 for _ in range(8)]
    for i in range(8):
        for t in range(4):
            first = pltpu.roll(got[t], (-(8 * i + 7)) % 128, 1)
            last = pltpu.roll(got[t], (63 - 8 * i) % 128, 1)
            tile = v_ref[i, 8 * t : 8 * t + 8, :]
            tile = tile + jnp.where(lane == 0, first, 0.0) + jnp.where(lane == 127, last, 0.0)
            own[i][t] = tile
            field[32 * i + 8 * t : 32 * i + 8 * t + 8, :] = tile
        v0_ref[i, 0:8, :] = own[i][1]
        v0_ref[i, 8:16, :] = own[i][2]
    for t in range(4):
        field[256 + 8 * t : 264 + 8 * t, :] = halo[t]
    along_k = dot(field[...], kk_ref[...])
    along_j = dot(kr_ref[...], field[0:256, :])
    halo_j = dot(kr_ref[0:32, 0:32], field[256:288, :])
    halo_i = dot(field[256:288, :], ki_ref[...])

    geo = g_ref[...]
    geo_halo = low_ref[32:48, :] + high_ref[32:48, :]
    out = [[None] * 4 for _ in range(8)]
    out_halo = []
    for t in range(4):
        g0, g1, g2, g3 = [node_rows(geo, d, t) for d in range(4)]
        f0, f1, f2, f3 = g0 * wj * wk, g1 * wk, g2 * wj, 50.0 * g3 * wj * wk
        if t in (1, 2):
            for d, f in enumerate((f0, f1, f2, f3)):
                maps_ref[d, 8 * t - 8 : 8 * t, :] = f
        for i in range(8):
            along_i = own[0][t] * float(STIFF[i, 0])
            for q in range(1, 8):
                along_i = along_i + own[q][t] * float(STIFF[i, q])
            at = slice(32 * i + 8 * t, 32 * i + 8 * t + 8)
            inner = f1 * along_j[at, :] + f2 * along_k[at, :] + f3 * own[i][t]
            out[i][t] = f0 * along_i + float(WEIGHTS[i]) * inner
        h0, h1, h2, h3 = [node_rows(geo_halo, d, t) for d in range(4)]
        at = slice(8 * t, 8 * t + 8)
        total = h0 * wj * wk * halo_i[at, :] + h1 * wi * wk * halo_j[at, :]
        total = total + h2 * wi * wj * along_k[256 + 8 * t : 264 + 8 * t, :]
        out_halo.append(total + 50.0 * h3 * wi * wj * wk * halo[t])

    row = row_ids()

    def middle(tiles):
        low, a, b, high = tiles
        new_a = a + jnp.where(row == 0, pltpu.roll(low, 1, 0), 0.0) + jnp.where(row == 7, pltpu.roll(b, 7, 0), 0.0)
        new_b = b + jnp.where(row == 0, pltpu.roll(a, 1, 0), 0.0) + jnp.where(row == 7, pltpu.roll(high, 7, 0), 0.0)
        return new_a, new_b

    beside = middle(out_halo)
    for i in range(8):
        local_ref[i, 0:8, :] = out[i][1]
        local_ref[i, 8:16, :] = out[i][2]
        for b, tile in enumerate(middle(out[i])):
            tile = join_lanes(tile)
            first = pltpu.roll(beside[b], (-(8 * i + 7)) % 128, 1)
            last = pltpu.roll(beside[b], (63 - 8 * i) % 128, 1)
            tile = tile + jnp.where(lane == 0, first, 0.0) + jnp.where(lane == 127, last, 0.0)
            part_ref[i, 8 * b : 8 * b + 8, :] = tile
            if i == 7:
                top_ref[8 * b : 8 * b + 8, :] = tile
            if i == 0:
                bottom_ref[8 * b : 8 * b + 8, :] = tile


def share_maps():
    s, v, w = [lax.axis_index(a) for a in AXES]
    row, lane = row_ids(), lane_ids()
    k = lane % 8
    shared = ((k == 0) & ((lane > 0) | (w > 0))) | ((k == 7) & ((lane < 127) | (w < 3)))
    span = jnp.where(shared, 0.5, 1.0)
    first = ((row == 0) & (v > 0)) | (row == 7)
    second = (row == 0) | ((row == 7) & (v < 7))
    tiles = (jnp.where(first, 0.5, 1.0) * span, jnp.where(second, 0.5, 1.0) * span)
    low = jnp.where(s > 0, 0.5, 1.0)
    high = jnp.where(s < 15, 0.5, 1.0)
    return tiles, [low] + [1.0] * 6 + [high]


def face_tiles(tiles):
    lane, row = lane_ids(), row_ids()
    out = []
    for side in range(2):
        out += [tiles[7 * side][0], tiles[7 * side][1]]
    for side in range(2):
        for b in range(2):
            tile = jnp.zeros((8, 128), F32)
            for i in range(8):
                tile = jnp.where(row == i, pltpu.roll(tiles[i][b], (i - 7 * side) % 8, 0), tile)
            out.append(tile)
    for side in range(2):
        for b in range(2):
            tile = jnp.zeros((8, 128), F32)
            for i in range(8):
                tile = jnp.where(lane % 8 == i, pltpu.roll(tiles[i][b], (i - 7 * side) % 128, 1), tile)
            out.append(tile)
    return out


def load_rows(faces, omega_ref):
    sums = [[None] * 4 for _ in range(6)]
    for d in range(3):
        targets = [(d, 1.0)] + [(3 + c, sign) for c, _, sign in MOMENTS[d]]
        for q, (component, sign) in enumerate(targets):
            for store in range(4):
                total = None
                for face in (2 * d, 2 * d + 1):
                    for b in range(2):
                        term = omega_ref[((2 * face + b) * 5 + store) * 3 + q] * faces[2 * face + b]
                        total = term if total is None else total + term
                total = total * sign
                before = sums[component][store]
                sums[component][store] = total if before is None else before + total
    return [jnp.sum(sums[c][s], axis=0, keepdims=True) for c in range(6) for s in range(4)]


def zero_rows(n):
    return [jnp.zeros((n, 128), F32)]


def sublane_sum(tile):
    return jnp.sum(tile, axis=0, keepdims=True)


def before_image(v0_ref, local_ref, part_ref, omega_ref, pre_ref):
    share, layers = share_maps()
    norm = energy = top = bottom = jnp.zeros((8, 128), F32)
    tiles = [[v0_ref[i, 0:8, :], v0_ref[i, 8:16, :]] for i in range(8)]
    for i in range(8):
        for b in range(2):
            x = tiles[i][b]
            square = x * x * share[b]
            norm = norm + square * layers[i]
            energy = energy + x * local_ref[i, 8 * b : 8 * b + 8, :]
            if 0 < i < 7:
                bottom = bottom + square
                top = top + x * part_ref[i, 8 * b : 8 * b + 8, :] * share[b]
    rows = [sublane_sum(norm), sublane_sum(energy)] + zero_rows(6)
    rows += load_rows(face_tiles(tiles), omega_ref)
    rows += [sublane_sum(top), sublane_sum(bottom)] + zero_rows(94)
    sums = lane_sums(jnp.concatenate(rows, axis=0))
    lane = lane_ids()
    over, under = sums[:, 32:33], sums[:, 33:34]
    usable = under > 1e-30
    quotient = jnp.where(usable, over / jnp.where(usable, under, 1.0), 0.0)
    quotient = jnp.broadcast_to(jnp.clip(quotient, 0.0, 1e6), (8, 128))
    pre_ref[...] = jnp.where(lane == 2, quotient, jnp.where(lane < 32, sums, 0.0))


def image_sums(
    v0_ref, local_ref, part_ref, low_ref, high_ref, maps_ref, omega_ref, pre_ref, kk_ref, kr_ref,
    v1_ref, out_ref, field,
):
    share, layers = share_maps()
    quotient = jnp.broadcast_to(pre_ref[:, 2:3], (8, 128))
    v1 = [[None] * 2 for _ in range(8)]
    u = [[None] * 2 for _ in range(8)]
    norm = cross_norm = energy = cross_energy = jnp.zeros((8, 128), F32)
    for i in range(8):
        for b in range(2):
            rows = slice(8 * b, 8 * b + 8)
            tile = part_ref[i, rows, :]
            if i == 0:
                tile = tile + low_ref[rows, :]
            if i == 7:
                tile = tile + high_ref[rows, :]
            v1[i][b] = tile
            v1_ref[i, rows, :] = tile
            x = v0_ref[i, rows, :]
            y = tile - quotient * x
            u[i][b] = y
            field[16 * i + 8 * b : 16 * i + 8 * b + 8, :] = y
            weighted = y * share[b] * layers[i]
            norm = norm + y * weighted
            cross_norm = cross_norm + x * weighted
            cross_energy = cross_energy + y * local_ref[i, rows, :]
    along_k = dot(field[...], kk_ref[...])
    along_j = dot(kr_ref[0:128, 0:128], field[...])
    for b in range(2):
        rows = slice(8 * b, 8 * b + 8)
        f0, f1, f2, f3 = [maps_ref[d, rows, :] for d in range(4)]
        for i in range(8):
            along_i = u[0][b] * float(STIFF[i, 0])
            for q in range(1, 8):
                along_i = along_i + u[q][b] * float(STIFF[i, q])
            at = slice(16 * i + 8 * b, 16 * i + 8 * b + 8)
            inner = f1 * along_j[at, :] + f2 * along_k[at, :] + f3 * u[i][b]
            energy = energy + u[i][b] * (f0 * along_i + float(WEIGHTS[i]) * inner)
    rows = zero_rows(3) + [sublane_sum(a) for a in (norm, cross_norm, energy, cross_energy)] + zero_rows(25)
    rows += load_rows(face_tiles(v1), omega_ref) + zero_rows(72)
    sums = lane_sums(jnp.concatenate(rows, axis=0)) + pre_ref[...]
    out_ref[...] = jnp.broadcast_to(sums[0:1, :][None], (32, 1, 128))


def merged(parts, last):
    m, q, s, uu, g, ulu, t = [parts[:, n : n + 1] for n in range(7)]

    def add(a):
        return jnp.sum(a, axis=0, keepdims=True)

    m_all, q_all = add(m), add(q)
    if last:
        common = q_all / m_all
    else:
        usable = m_all > 0.0
        common = jnp.where(usable, add(m * s) / jnp.where(usable, m_all, 1.0), 0.0)
    e = s - common
    uu_all = add(uu + e * (2.0 * g + e * m))
    g_all = add(g + e * m)
    ulu_all = add(ulu + e * (2.0 * t + e * q))
    t_all = add(t + e * q)
    return m_all, q_all, common, uu_all, g_all, ulu_all, t_all, add(parts)


def group_sums(parts_ref, out_ref):
    parts = parts_ref[...].reshape(parts_ref.shape[0], 128)
    values = merged(parts, False)
    row = values[7]
    lane = lane_ids(1)
    for n in range(7):
        row = jnp.where(lane == n, values[n], row)
    out_ref[...] = jnp.broadcast_to(row[None], out_ref.shape)


def finish(parts_ref, v0_ref, v1_ref, arm_ref, store_ref, motion_ref, p_ref, velocity_ref):
    parts = parts_ref[...].reshape(parts_ref.shape[0], 128)
    m, q, _, uu, _, ulu, _, sums = merged(parts, True)
    alpha = m / q
    beta = alpha * alpha * uu / m
    new = alpha * alpha * uu
    curve = alpha * alpha * ulu - beta * beta * q
    alpha_next = new / curve
    c0 = alpha + alpha_next * (1.0 + beta)
    c1 = -alpha_next * alpha
    for i in range(8):
        p_ref[i] = c0 * v0_ref[i] + c1 * v1_ref[i]
    loads = c0 * sums + c1 * pltpu.roll(sums, 104, 1)
    state = motion_ref[0:1, :] + motion_ref[1:2, :] * loads
    stores = store_ref[...]
    zero = jnp.zeros((32, 128), F32)
    maps = []
    for c in range(6):
        total = zero
        for store in range(4):
            at = 8 + 4 * c + store
            total = jnp.where(stores == store, state[:, at : at + 1], total)
        maps.append(total)
    arms = [arm_ref[c] for c in range(3)]
    for c in range(3):
        a, b = (c + 1) % 3, (c + 2) % 3
        value = maps[c] + (maps[3 + a] * arms[b] - maps[3 + b] * arms[a])
        for r in range(32):
            velocity_ref[0, c : c + 1, 128 * r : 128 * r + 128] = value[r : r + 1, :]


def wall_weights(elem_ref, face_ref, store_ref, node_ref, spread_ref, omega_ref, spread):
    spread[...] = dot(node_ref[...], spread_ref[...])
    omega_ref[...] = jnp.zeros(omega_ref.shape, F32)
    lane = lane_ids() // 8

    def add(n, carry):
        elem, face, store = elem_ref[0, n], face_ref[0, n], store_ref[0, n]
        tile = (2 * face + elem // 16) * 5 + store
        here = lane == elem % 16
        for q in range(3):
            at = pl.multiple_of((q * 64 + n) * 8, 8)
            omega_ref[tile * 3 + q] += jnp.where(here, spread[pl.ds(at, 8), :], 0.0)
        return carry

    lax.fori_loop(0, 64, add, 0)


def shifted(x, axis, step, ring=False):
    count = lax.axis_size(axis)
    pairs = [(i, (i + step) % count) for i in range(count) if ring or 0 <= i + step < count]
    return lax.ppermute(x, axis, pairs)


def per_device(
    forcing, geometry, wall_elem, wall_face, wall_store, wall_weight, wall_arm, store_motion, store_inverse
):
    lane_k, lane_i, rows, node_w = [jnp.asarray(a) for a in constants()]
    field = (8, 16, 128)

    low = shifted(forcing[7], "stream", 1)
    high = shifted(forcing[0], "stream", -1)

    geo = jnp.repeat(geometry.reshape(8, 16), 8, axis=1)
    face = wall_face[0]
    sign = (1 - 2 * (face % 2)).astype(F32)[:, None]
    weight = wall_weight[0].reshape(64, 64) * sign
    arms = wall_arm[0].reshape(3, 64, 64)
    direction = (face // 2)[:, None]
    first = jnp.where(direction == 2, arms[1], arms[2])
    second = jnp.where(direction == 0, arms[1], arms[0])
    nodes = jnp.stack([weight, weight * first, weight * second]).reshape(3, 64, 8, 8)
    nodes = jnp.where((direction == 2)[None, :, :, None], jnp.swapaxes(nodes, 2, 3), nodes)
    spread = jnp.asarray(np.kron(np.ones((1, 16)), np.eye(8)).astype(np.float32))
    omega = call(wall_weights, [(180, 8, 128)], cost=4000, scratch_shapes=[pltpu.VMEM((1536, 128), F32)])(
        wall_elem, wall_face, wall_store, nodes.reshape(1536, 8), spread, smem=3
    )[0]
    arm_rows = wall_arm[0].reshape(3, 32, 128)
    store_rows = jnp.repeat(wall_store[0], 64).reshape(32, 128)
    zeros8, zeros96 = jnp.zeros((8,), F32), jnp.zeros((96,), F32)
    scale = jnp.concatenate([store_inverse[0:1]] * 3 + [store_inverse[1:4]], axis=0)
    motion = jnp.stack(
        [
            jnp.concatenate([zeros8, store_motion.reshape(24), zeros96]),
            jnp.concatenate([zeros8, scale.reshape(24), zeros96]),
        ]
    )

    x, up, down = call(stream_added, [field, (72, 128), (72, 128)])(forcing, low, high, geo)
    low = shifted(up, "vert", 1, ring=True)
    high = shifted(down, "vert", -1, ring=True)
    wide, geo_wide, right, left = call(vert_added, [(8, 32, 128), (16, 128), (48, 128), (48, 128)])(
        x, low, high, geo
    )
    low = shifted(right, "span", 1)
    high = shifted(left, "span", -1)
    v0, local, part, top, bottom, maps = call(
        span_added,
        [field, field, field, (16, 128), (16, 128), (4, 16, 128)],
        scratch_shapes=[pltpu.VMEM((288, 128), F32)],
    )(wide, geo_wide, right, left, low, high, lane_k, lane_i, rows, node_w)
    low = shifted(top, "stream", 1)
    high = shifted(bottom, "stream", -1)
    pre = call(before_image, [(8, 128)])(v0, local, part, omega)[0]
    v1, sums = call(image_sums, [field, (32, 1, 128)], scratch_shapes=[pltpu.VMEM((128, 128), F32)])(
        v0, local, part, low, high, maps, omega, pre, lane_k, rows
    )
    sums = lax.all_to_all(sums, ("vert", "span"), 0, 0)
    sums = call(group_sums, [(16, 1, 128)])(sums)[0]
    sums = lax.all_to_all(sums, "stream", 0, 0)
    pressure, velocity = call(finish, [field, (1, 3, 4096)])(sums, v0, v1, arm_rows, store_rows, motion)
    return pressure, velocity


def solution(mesh):
    return jax.shard_map(
        per_device,
        mesh=mesh,
        in_specs=(
            P("stream", "vert", "span"),
            P(None, "stream", "vert", "span"),
            SHARDS,
            SHARDS,
            SHARDS,
            SHARDS,
            P(AXES, None, None),
            P(),
            P(),
        ),
        out_specs=(P("stream", "vert", "span"), P(AXES, None, None)),
        check_vma=False,
    )
```

```python
import functools

import jax
import jax.numpy as jnp
import numpy as np
from jax import lax
from jax.experimental import pallas as pl
from jax.experimental.pallas import tpu as pltpu
from jax.sharding import PartitionSpec as P

F32 = jnp.float32
UU, G2, M, ULU, T2, Q, S = range(7)
AXES = ("stream", "vert", "span")
SHARDS = P(AXES, None)
gll_inner = [
    -0.8717401485096066,
    -0.5917001814331423,
    -0.2092992179024789,
    0.2092992179024789,
    0.5917001814331423,
    0.8717401485096066,
]
MOMENTS = (((1, 2, 1.0), (2, 1, -1.0)), ((0, 2, -1.0), (2, 0, 1.0)), ((0, 1, 1.0), (1, 0, -1.0)))


def legendre_seven(points):
    before = points * 0.0 + 1.0
    current = points * 1.0
    for order in range(1, 7):
        following = ((2 * order + 1) * points * current - order * before) / (order + 1)
        before = current
        current = following
    return current


def gll_tables():
    degree = 7
    points = np.array([-1.0] + gll_inner + [1.0])
    legendre_at = legendre_seven(points)
    weights = 2.0 / (degree * (degree + 1) * legendre_at**2)
    derivative = np.zeros((8, 8))
    for i in range(8):
        for j in range(8):
            if i != j:
                derivative[i, j] = legendre_at[i] / (legendre_at[j] * (points[i] - points[j]))
    derivative[0, 0] = -degree * (degree + 1) / 4.0
    derivative[7, 7] = degree * (degree + 1) / 4.0
    return derivative, weights


DERIV, WEIGHTS = gll_tables()
STIFF = DERIV.T @ np.diag(WEIGHTS) @ DERIV


def constants():
    def f32(a):
        return np.asarray(a, np.float32)

    lane_k = f32(np.kron(np.eye(16), STIFF))
    lane_i = f32(np.kron(np.eye(2), np.kron(STIFF, np.eye(8))))
    rows = f32(np.kron(np.eye(32), STIFF))
    wj = np.tile(WEIGHTS[:, None], (1, 128))
    wk = np.tile(np.tile(WEIGHTS, 16)[None], (8, 1))
    wi = np.tile(np.tile(np.repeat(WEIGHTS, 8), 2)[None], (8, 1))
    return lane_k, lane_i, rows, f32(np.concatenate([wj, wk, wi], axis=0))


def dot(a, b):
    return lax.dot_general(
        a,
        b,
        (((1,), (0,)), ((), ())),
        precision=lax.Precision.HIGHEST,
        preferred_element_type=F32,
    )


def lane_sums(rows, first):
    n = rows.shape[0]
    sums = jnp.sum(rows, axis=1, keepdims=True)
    place = lax.broadcasted_iota(jnp.int32, (n, 128), 0) + first
    return jnp.sum(jnp.where(lane_ids(n) == place, sums, 0.0), axis=0, keepdims=True)


def row_ids():
    return lax.broadcasted_iota(jnp.int32, (8, 128), 0)


def lane_ids(rows=8):
    return lax.broadcasted_iota(jnp.int32, (rows, 128), 1)


def join_rows(below, above):
    row = row_ids()
    new_below = below + jnp.where(row == 7, pltpu.roll(above, 7, 0), 0.0)
    new_above = above + jnp.where(row == 0, pltpu.roll(below, 1, 0), 0.0)
    return new_below, new_above


def join_lanes(tile):
    lane = lane_ids()
    k = lane % 8
    left = jnp.where((k == 0) & (lane > 0), pltpu.roll(tile, 1, 1), 0.0)
    right = jnp.where((k == 7) & (lane < 127), pltpu.roll(tile, 127, 1), 0.0)
    return tile + left + right


def call(body, outs, cost=2000, space=pltpu.VMEM, out_space=pltpu.VMEM, **kwargs):
    given, taken = pl.BlockSpec(memory_space=space), pl.BlockSpec(memory_space=out_space)

    shapes = [s if isinstance(s[0], tuple) else (s, F32) for s in outs]

    def run(*args, smem=0):
        specs = [pl.BlockSpec(memory_space=pltpu.SMEM)] * smem + [given] * (len(args) - smem)
        return pl.pallas_call(
            body,
            out_shape=[jax.ShapeDtypeStruct(*s) for s in shapes],
            in_specs=specs,
            out_specs=[taken] * len(outs),
            compiler_params=pltpu.CompilerParams(vmem_limit_bytes=16 * 2**20),
            cost_estimate=pl.CostEstimate(flops=cost * 1000, bytes_accessed=200000, transcendentals=0),
            **kwargs,
        )(*args)

    return run


def stream_added(f_ref, low_ref, high_ref, geo_ref, x_ref, up_ref, down_ref):
    low, high = in_order(low_ref[...], high_ref[...], "A" in SWAPS)
    for i in range(8):
        a = f_ref[i, 0:8, :]
        b = f_ref[i, 8:16, :]
        if i == 0:
            a = a + low[0:8, :]
            b = b + low[8:16, :]
        if i == 7:
            a = a + high[0:8, :]
            b = b + high[8:16, :]
        a, b = join_rows(a, b)
        x_ref[i, 0:8, :] = a
        x_ref[i, 8:16, :] = b
        down_ref[8 * i : 8 * i + 8, :] = a
        up_ref[8 * i : 8 * i + 8, :] = b
    down_ref[64:72, :] = geo_ref[...]
    up_ref[64:72, :] = geo_ref[...]


def vert_added(x_ref, low_ref, high_ref, geo_ref, v_ref, g_ref, right_ref, left_ref):
    v = lax.axis_index("vert")
    has_low = jnp.where(v > 0, 1.0, 0.0)
    has_high = jnp.where(v < 7, 1.0, 0.0)
    lane = lane_ids()
    right = [jnp.zeros((8, 128), F32) for _ in range(4)]
    left = [jnp.zeros((8, 128), F32) for _ in range(4)]
    for i in range(8):
        rows = slice(8 * i, 8 * i + 8)
        low, a = join_rows(low_ref[rows, :] * has_low, x_ref[i, 0:8, :])
        b, high = join_rows(x_ref[i, 8:16, :], high_ref[rows, :] * has_high)
        for t, tile in enumerate((low, a, b, high)):
            tile = join_lanes(tile)
            v_ref[i, 8 * t : 8 * t + 8, :] = tile
            to_right = pltpu.roll(tile, (8 * i - 120) % 128, 1)
            to_left = pltpu.roll(tile, 64 + 8 * i, 1)
            right[t] = jnp.where(lane // 8 == i, to_right, right[t])
            left[t] = jnp.where(lane // 8 == 8 + i, to_left, left[t])
    for t in range(4):
        right_ref[8 * t : 8 * t + 8, :] = right[t]
        left_ref[8 * t : 8 * t + 8, :] = left[t]
    geo = geo_ref[...]
    geo_low = low_ref[64:72, :] * has_low
    geo_high = high_ref[64:72, :] * has_high
    rows = []
    for d in range(4):
        rows.append(geo_low[2 * d + 1 : 2 * d + 2, :])
        rows.append(geo[2 * d : 2 * d + 2, :])
        rows.append(geo_high[2 * d : 2 * d + 1, :])
    extended = jnp.concatenate(rows, axis=0)
    g_ref[...] = extended
    wide = lane_ids(16)
    last = jnp.broadcast_to(extended[:, 127:128], (16, 128))
    first = jnp.broadcast_to(extended[:, 0:1], (16, 128))
    right_ref[32:48, :] = jnp.where(wide < 64, last, 0.0)
    left_ref[32:48, :] = jnp.where(wide >= 64, first, 0.0)


def node_rows(geo, d, t):
    return jnp.broadcast_to(geo[4 * d + t : 4 * d + t + 1, :], (8, 128))


def span_added(
    v_ref, g_ref, right_ref, left_ref, low_ref, high_ref, kk_ref, ki_ref, kr_ref, w_ref,
    v0_ref, local_ref, part_ref, top_ref, bottom_ref, maps_ref, field,
):
    lane = lane_ids()
    wj, wk, wi = w_ref[0:8, :], w_ref[8:16, :], w_ref[16:24, :]
    got = [low_ref[8 * t : 8 * t + 8, :] + high_ref[8 * t : 8 * t + 8, :] for t in range(4)]
    halo = []
    for t in range(4):
        rows = slice(8 * t, 8 * t + 8)
        from_own_first = pltpu.roll(left_ref[rows, :], 71, 1)
        from_own_last = pltpu.roll(right_ref[rows, :], 57, 1)
        tile = got[t] + jnp.where((lane < 64) & (lane % 8 == 7), from_own_first, 0.0)
        halo.append(tile + jnp.where((lane >= 64) & (lane % 8 == 0), from_own_last, 0.0))
    own = [[None] * 4 for _ in range(8)]
    for i in range(8):
        for t in range(4):
            first = pltpu.roll(got[t], (-(8 * i + 7)) % 128, 1)
            last = pltpu.roll(got[t], (63 - 8 * i) % 128, 1)
            tile = v_ref[i, 8 * t : 8 * t + 8, :]
            tile = tile + jnp.where(lane == 0, first, 0.0) + jnp.where(lane == 127, last, 0.0)
            own[i][t] = tile
            field[32 * i + 8 * t : 32 * i + 8 * t + 8, :] = tile
        v0_ref[i, 0:8, :] = own[i][1]
        v0_ref[i, 8:16, :] = own[i][2]
    for t in range(4):
        field[256 + 8 * t : 264 + 8 * t, :] = halo[t]
    along_k = dot(field[...], kk_ref[...])
    along_j = dot(kr_ref[...], field[0:256, :])
    halo_j = dot(kr_ref[0:32, 0:32], field[256:288, :])
    halo_i = dot(field[256:288, :], ki_ref[...])

    geo = g_ref[...]
    geo_halo = low_ref[32:48, :] + high_ref[32:48, :]
    out = [[None] * 4 for _ in range(8)]
    out_halo = []
    for t in range(4):
        g0, g1, g2, g3 = [node_rows(geo, d, t) for d in range(4)]
        f0, f1, f2, f3 = g0 * wj * wk, g1 * wk, g2 * wj, 50.0 * g3 * wj * wk
        if t in (1, 2):
            for d, f in enumerate((f0, f1, f2, f3)):
                maps_ref[d, 8 * t - 8 : 8 * t, :] = f
        for i in range(8):
            along_i = own[0][t] * float(STIFF[i, 0])
            for q in range(1, 8):
                along_i = along_i + own[q][t] * float(STIFF[i, q])
            at = slice(32 * i + 8 * t, 32 * i + 8 * t + 8)
            inner = f1 * along_j[at, :] + f2 * along_k[at, :] + f3 * own[i][t]
            out[i][t] = f0 * along_i + float(WEIGHTS[i]) * inner
        h0, h1, h2, h3 = [node_rows(geo_halo, d, t) for d in range(4)]
        at = slice(8 * t, 8 * t + 8)
        total = h0 * wj * wk * halo_i[at, :] + h1 * wi * wk * halo_j[at, :]
        total = total + h2 * wi * wj * along_k[256 + 8 * t : 264 + 8 * t, :]
        out_halo.append(total + 50.0 * h3 * wi * wj * wk * halo[t])

    row = row_ids()

    def middle(tiles):
        low, a, b, high = tiles
        new_a = a + jnp.where(row == 0, pltpu.roll(low, 1, 0), 0.0) + jnp.where(row == 7, pltpu.roll(b, 7, 0), 0.0)
        new_b = b + jnp.where(row == 0, pltpu.roll(a, 1, 0), 0.0) + jnp.where(row == 7, pltpu.roll(high, 7, 0), 0.0)
        return new_a, new_b

    beside = middle(out_halo)
    outer = {0: [], 7: []}
    for i in range(8):
        local_ref[i, 0:8, :] = out[i][1]
        local_ref[i, 8:16, :] = out[i][2]
        for b, tile in enumerate(middle(out[i])):
            tile = join_lanes(tile)
            first = pltpu.roll(beside[b], (-(8 * i + 7)) % 128, 1)
            last = pltpu.roll(beside[b], (63 - 8 * i) % 128, 1)
            tile = tile + jnp.where(lane == 0, first, 0.0) + jnp.where(lane == 127, last, 0.0)
            part_ref[i, 8 * b : 8 * b + 8, :] = tile
            if i in (0, 7):
                outer[i].append(tile)
    top, bottom = [jnp.concatenate(outer[i], axis=0) for i in (7, 0)]
    bottom_ref[...], top_ref[...] = in_order(bottom, top, "D" in SWAPS)


def share_maps():
    s, v, w = [lax.axis_index(a) for a in AXES]
    row, lane = row_ids(), lane_ids()
    k = lane % 8
    shared = ((k == 0) & ((lane > 0) | (w > 0))) | ((k == 7) & ((lane < 127) | (w < 3)))
    span = jnp.where(shared, 0.5, 1.0)
    first = ((row == 0) & (v > 0)) | (row == 7)
    second = (row == 0) | ((row == 7) & (v < 7))
    tiles = (jnp.where(first, 0.5, 1.0) * span, jnp.where(second, 0.5, 1.0) * span)
    low = jnp.where(s > 0, 0.5, 1.0)
    high = jnp.where(s < 15, 0.5, 1.0)
    return tiles, [low] + [1.0] * 6 + [high]


def face_tiles(tiles):
    lane, row = lane_ids(), row_ids()
    out = []
    for side in range(2):
        out += [tiles[7 * side][0], tiles[7 * side][1]]
    for side in range(2):
        for b in range(2):
            tile = jnp.zeros((8, 128), F32)
            for i in range(8):
                tile = jnp.where(row == i, pltpu.roll(tiles[i][b], (i - 7 * side) % 8, 0), tile)
            out.append(tile)
    for side in range(2):
        for b in range(2):
            tile = jnp.zeros((8, 128), F32)
            for i in range(8):
                tile = jnp.where(lane % 8 == i, pltpu.roll(tiles[i][b], (i - 7 * side) % 128, 1), tile)
            out.append(tile)
    return [tile if (n // 2) % 2 == 0 else -tile for n, tile in enumerate(out)]


def load_rows(faces, omega_ref):
    sums = [[None] * 4 for _ in range(6)]
    for d in range(3):
        targets = [(d, 1.0)] + [(3 + c, sign) for c, _, sign in MOMENTS[d]]
        for q, (component, sign) in enumerate(targets):
            for store in range(4):
                total = None
                for face in (2 * d, 2 * d + 1):
                    for b in range(2):
                        term = omega_ref[((2 * face + b) * 5 + store) * 3 + q] * faces[2 * face + b]
                        total = term if total is None else total + term
                total = total * sign
                before = sums[component][store]
                sums[component][store] = total if before is None else before + total
    return [jnp.sum(sums[c][s], axis=0, keepdims=True) for c in range(6) for s in range(4)]


def zero_rows(n):
    return [jnp.zeros((n, 128), F32)]


def sublane_sum(tile):
    return jnp.sum(tile, axis=0, keepdims=True)


def before_image(v0_ref, local_ref, part_ref, omega_ref, pre_ref):
    share, layers = share_maps()
    norm = energy = top = bottom = jnp.zeros((8, 128), F32)
    tiles = [[v0_ref[i, 0:8, :], v0_ref[i, 8:16, :]] for i in range(8)]
    for i in range(8):
        for b in range(2):
            x = tiles[i][b]
            square = x * x * share[b]
            norm = norm + square * layers[i]
            energy = energy + x * local_ref[i, 8 * b : 8 * b + 8, :]
            if 0 < i < 7:
                bottom = bottom + square
                top = top + x * part_ref[i, 8 * b : 8 * b + 8, :] * share[b]
    rows = [sublane_sum(top), sublane_sum(norm), sublane_sum(bottom)] + zero_rows(1)
    rows += [sublane_sum(energy)] + zero_rows(3) + load_rows(face_tiles(tiles), omega_ref)
    sums = lane_sums(jnp.concatenate(rows, axis=0), 0)
    lane = lane_ids(1)
    over, norm, under, energy = sums[:, 0:1], sums[:, 1:2], sums[:, 2:3], sums[:, 4:5]
    usable = under > 1e-30
    quotient = jnp.where(usable, over / jnp.where(usable, under, 1.0), 0.0)
    quotient = jnp.clip(quotient, 0.0, 1e6)
    row = jnp.where(lane >= 8, sums, 0.0)
    for n, value in ((M, norm), (Q, energy), (S, quotient)):
        row = jnp.where(lane == n, value, row)
    pre_ref[...] = jnp.broadcast_to(row, (8, 128))


def image_sums(
    v0_ref, local_ref, part_ref, low_ref, high_ref, maps_ref, omega_ref, pre_ref, kk_ref, kr_ref,
    v1_ref, out_ref, field,
):
    share, layers = share_maps()
    low, high = in_order(low_ref[...], high_ref[...], "D" in SWAPS)
    quotient = jnp.broadcast_to(pre_ref[:, S : S + 1], (8, 128))
    v1 = [[None] * 2 for _ in range(8)]
    u = [[None] * 2 for _ in range(8)]
    norm = cross_norm = energy = cross_energy = jnp.zeros((8, 128), F32)
    for i in range(8):
        for b in range(2):
            rows = slice(8 * b, 8 * b + 8)
            tile = part_ref[i, rows, :]
            if i == 0:
                tile = tile + low[rows, :]
            if i == 7:
                tile = tile + high[rows, :]
            v1[i][b] = tile
            v1_ref[i, rows, :] = tile
            x = v0_ref[i, rows, :]
            y = tile - quotient * x
            u[i][b] = y
            field[16 * i + 8 * b : 16 * i + 8 * b + 8, :] = y
            weighted = y * share[b] * layers[i]
            norm = norm + y * weighted
            cross_norm = cross_norm + x * weighted
            cross_energy = cross_energy + y * local_ref[i, rows, :]
    along_k = dot(field[...], kk_ref[...])
    along_j = dot(kr_ref[0:128, 0:128], field[...])
    for b in range(2):
        rows = slice(8 * b, 8 * b + 8)
        f0, f1, f2, f3 = [maps_ref[d, rows, :] for d in range(4)]
        for i in range(8):
            along_i = u[0][b] * float(STIFF[i, 0])
            for q in range(1, 8):
                along_i = along_i + u[q][b] * float(STIFF[i, q])
            at = slice(16 * i + 8 * b, 16 * i + 8 * b + 8)
            inner = f1 * along_j[at, :] + f2 * along_k[at, :] + f3 * u[i][b]
            energy = energy + u[i][b] * (f0 * along_i + float(WEIGHTS[i]) * inner)
    rows = [sublane_sum(a) for a in (norm, 2.0 * cross_norm)] + zero_rows(1)
    rows += [sublane_sum(a) for a in (energy, 2.0 * cross_energy)] + zero_rows(3)
    row = lane_sums(jnp.concatenate(rows, axis=0), 0)
    row = row + lane_sums(jnp.concatenate(load_rows(face_tiles(v1), omega_ref), axis=0), 32)
    out_ref[...] = jnp.broadcast_to(row + pre_ref[0:1, :], (32, 128))


def merged(parts):
    n = parts.shape[0]
    lane = lane_ids(n)
    common = parts[0:1, S : S + 1]
    e = parts[:, S : S + 1] - common
    once = jnp.where((lane == UU) | (lane == ULU), 1.0, jnp.where((lane == G2) | (lane == T2), 2.0, 0.0))
    twice = jnp.where((lane == UU) | (lane == ULU), 1.0, 0.0)
    rows = parts + e * (once * pltpu.roll(parts, 127, 1) + e * (twice * pltpu.roll(parts, 126, 1)))
    total = jnp.sum(rows, axis=0, keepdims=True)
    return jnp.where(lane_ids(1) == S, common, total)


def group_sums(parts_ref, out_ref):
    out_ref[...] = jnp.broadcast_to(merged(parts_ref[...]), out_ref.shape)


def finish(
    parts_ref, v0_ref, v1_ref, arm_ref, store_ref, motion_ref, p_out, velocity_out, p_ref, velocity_ref, sems
):
    total = merged(parts_ref[...])
    uu, g2, m, ulu, t2, q, s = [total[:, n : n + 1] for n in range(7)]
    alpha = m / q
    e = s - q / m
    uu = uu + e * (g2 + e * m)
    ulu = ulu + e * (t2 + e * q)
    square = alpha * alpha
    beta = square * uu / m
    curve = square * ulu - beta * beta * q
    alpha_next = square * uu / curve
    c0 = alpha + alpha_next * (1.0 + beta)
    c1 = -alpha_next * alpha
    wide0 = jnp.broadcast_to(c0, (16, 128))
    wide1 = jnp.broadcast_to(c1, (16, 128))
    for i in range(8):
        p_ref[i] = wide0 * v0_ref[i] + wide1 * v1_ref[i]
    p_copy = pltpu.make_async_copy(p_ref, p_out, sems.at[0])
    p_copy.start()
    loads = c0 * total + c1 * pltpu.roll(total, 104, 1)
    state = motion_ref[0:1, :] + motion_ref[1:2, :] * loads
    stores = store_ref[...]
    maps = []
    for c in range(6):
        value = jnp.zeros((32, 128), F32)
        for store in range(4):
            at = 8 + 4 * c + store
            value = jnp.where(stores == store, state[:, at : at + 1], value)
        maps.append(value)
    arms = [arm_ref[c] for c in range(3)]
    for c in range(3):
        a, b = (c + 1) % 3, (c + 2) % 3
        velocity_ref[c] = maps[c] + (maps[3 + a] * arms[b] - maps[3 + b] * arms[a])
    velocity_copy = pltpu.make_async_copy(velocity_ref, velocity_out, sems.at[1])
    velocity_copy.start()
    p_copy.wait()
    velocity_copy.wait()


def spread_geometry(geo_ref, out_ref):
    element = lax.broadcasted_iota(jnp.int32, (16, 128), 0)
    out_ref[...] = dot(geo_ref[...], jnp.where((lane_ids(16) >> 3) == element, 1.0, 0.0))


def wall_table(
    elem_ref, face_ref, stores_ref, motion_ref, inverse_ref, weight_ref, arm_ref,
    table_ref, code_ref, store_out, motion_out,
):
    weight = weight_ref[...]
    nodes = jnp.concatenate([weight] + [weight * arm_ref[c] for c in range(3)], axis=0)
    a = lax.broadcasted_iota(jnp.int32, (128, 128), 0)
    b = lax.broadcasted_iota(jnp.int32, (128, 128), 1)
    slot, outer, inner = a & 64, (a >> 3) & 7, a & 7
    table_ref[0:128, :] = dot(nodes, jnp.where(b == slot + (7 - outer) * 8 + inner, 1.0, 0.0))
    table_ref[128:256, :] = dot(nodes, jnp.where(b == slot + (7 - inner) * 8 + outer, 1.0, 0.0))

    elem, face, stores = elem_ref[...], face_ref[...], stores_ref[...]
    n = lax.broadcasted_iota(jnp.int32, (1, 64), 1)
    direction = face >> 1
    first = jnp.where(direction == 2, 128, 0) + (n >> 1)
    column = elem & 15
    code_ref[0:1, :] = ((2 * face + (elem >> 4)) * 5 + stores) * 3
    code_ref[1:2, :] = column
    code_ref[2:3, :] = (8 * column + 64 * (n & 1) + 72) & 127
    code_ref[3:4, :] = first
    code_ref[4:5, :] = first + jnp.where(direction == 2, 64, 96)
    code_ref[5:6, :] = first + jnp.where(direction == 0, 64, 32)
    code_ref[6:8, :] = jnp.zeros((2, 64), jnp.int32)

    numbers = stores.astype(F32)
    row = lax.broadcasted_iota(jnp.int32, (32, 64), 0)
    column = lax.broadcasted_iota(jnp.int32, (32, 64), 1)
    even = jnp.sum(jnp.where(column == 2 * row, numbers, 0.0), axis=1, keepdims=True)
    odd = jnp.sum(jnp.where(column == 2 * row + 1, numbers, 0.0), axis=1, keepdims=True)
    store_out[...] = jnp.where(lane_ids(32) < 64, even, odd)

    load = lane_ids(8) - 8
    inside = (load >= 0) & (load < 24)
    component, store = load >> 2, load & 3
    row = row_ids()
    motion = dot(motion_ref[...], jnp.where(inside & (component == row), 1.0, 0.0)[0:6, :])
    motion_out[0:1, :] = jnp.sum(jnp.where((store == row)[0:4, :], motion, 0.0), axis=0, keepdims=True)
    scale = dot(inverse_ref[...], jnp.where(inside & (store == row), 1.0, 0.0)[0:4, :])
    taken = jnp.maximum(component - 2, 0) == row
    motion_out[1:2, :] = jnp.sum(jnp.where(taken[0:4, :], scale, 0.0), axis=0, keepdims=True)


def wall_weights(begin, end, code_ref, table_ref, *rest):
    omega_ref = rest[-1]
    if begin == 0:
        omega_ref[...] = jnp.zeros(omega_ref.shape, F32)
    lane = lane_ids() >> 3

    def add(step, carry):
        tiles = []
        for k in range(8):
            n = begin + 8 * step + k
            here = lane == code_ref[1, n]
            for q in range(3):
                nodes = jnp.broadcast_to(table_ref[pl.ds(code_ref[3 + q, n], 1), :], (8, 128))
                nodes = pltpu.roll(pltpu.roll(nodes, 0, 1, stride=8, stride_axis=0), code_ref[2, n], 1)
                tiles.append(jnp.where(here, nodes, 0.0))
        for k in range(8):
            at = code_ref[0, begin + 8 * step + k]
            for q in range(3):
                omega_ref[at + q] += tiles[3 * k + q]
        return carry

    lax.fori_loop(0, (end - begin) // 8, add, 0)


def shifted(x, axis, step, ring=False):
    count = lax.axis_size(axis)
    pairs = [(i, (i + step) % count) for i in range(count) if ring or 0 <= i + step < count]
    return lax.ppermute(x, axis, pairs)


def swapped(x, axis, first):
    pairs = [(i, i + 1) for i in range(first, lax.axis_size(axis) - 1, 2)]
    return lax.ppermute(x, axis, pairs + [(b, a) for a, b in pairs])


SWAPS = "A"


def stream_exchange(one, two, swap):
    if swap:
        return swapped(one, "stream", 0), swapped(two, "stream", 1)
    return shifted(one, "stream", 1), shifted(two, "stream", -1)


def in_order(first, second, swap):
    if not swap:
        return first, second
    even = lax.axis_index("stream") % 2 == 0
    return jnp.where(even, second, first), jnp.where(even, first, second)


def per_device(
    forcing, geometry, wall_elem, wall_face, wall_store, wall_weight, wall_arm, store_motion, store_inverse
):
    lane_k, lane_i, rows, node_w = [jnp.asarray(a) for a in constants()]
    field = (8, 16, 128)
    tie = lax.optimization_barrier

    if "A" in SWAPS:
        odd = lax.axis_index("stream") % 2
        top, bottom = [lax.dynamic_index_in_dim(forcing, at, 0, False) for at in (7 - 7 * odd, 7 * odd)]
    else:
        top, bottom = forcing[7], forcing[0]
    low, high = stream_exchange(top, bottom, "A" in SWAPS)
    geo = call(spread_geometry, [(8, 128)])(geometry.reshape(8, 16))[0]
    x, up, down = call(stream_added, [field, (72, 128), (72, 128)])(forcing, low, high, geo)

    up, down, weight, arms = tie((up, down, wall_weight.reshape(32, 128), wall_arm.reshape(3, 32, 128)))
    low = shifted(up, "vert", 1, ring=True)
    high = shifted(down, "vert", -1, ring=True)
    table, codes, store_rows, motion = call(
        wall_table, [(256, 128), ((8, 64), jnp.int32), (32, 128), (2, 128)]
    )(wall_elem, wall_face, wall_store, store_motion.T, store_inverse, weight, arms)
    low, high, table, codes = tie((low, high, table, codes))
    wide, geo_wide, right, left = call(vert_added, [(8, 32, 128), (16, 128), (48, 128), (48, 128)])(
        x, low, high, geo
    )

    right, left, table, codes = tie((right, left, table, codes))
    low = shifted(right, "span", 1)
    high = shifted(left, "span", -1)
    omega = call(functools.partial(wall_weights, 0, 64), [(180, 8, 128)])(codes, table, smem=1)[0]
    low, high, omega = tie((low, high, omega))
    v0, local, part, top, bottom, maps = call(
        span_added,
        [field, field, field, (16, 128), (16, 128), (4, 16, 128)],
        scratch_shapes=[pltpu.VMEM((288, 128), F32)],
    )(wide, geo_wide, right, left, low, high, lane_k, lane_i, rows, node_w)

    low, high = stream_exchange(top, bottom, "D" in SWAPS)
    pre = call(before_image, [(8, 128)])(v0, local, part, omega)[0]
    v1, sums = call(image_sums, [field, (32, 128)], scratch_shapes=[pltpu.VMEM((128, 128), F32)])(
        v0, local, part, low, high, maps, omega, pre, lane_k, rows
    )
    sums = lax.all_to_all(sums.reshape(32, 1, 128), ("vert", "span"), 0, 0)
    sums = call(group_sums, [(16, 128)])(sums.reshape(32, 128))[0]
    sums = lax.all_to_all(sums.reshape(16, 1, 128), "stream", 0, 0)
    pressure, velocity = call(
        finish,
        [field, (3, 32, 128)],
        out_space=pltpu.HBM,
        scratch_shapes=[pltpu.VMEM(field, F32), pltpu.VMEM((3, 32, 128), F32), pltpu.SemaphoreType.DMA((2,))],
    )(sums.reshape(16, 128), v0, v1, arms, store_rows, motion)
    return pressure, velocity.reshape(1, 3, 4096)


def solution(mesh):
    return jax.shard_map(
        per_device,
        mesh=mesh,
        in_specs=(
            P("stream", "vert", "span"),
            P(None, "stream", "vert", "span"),
            SHARDS,
            SHARDS,
            SHARDS,
            SHARDS,
            P(AXES, None, None),
            P(),
            P(),
        ),
        out_specs=(P("stream", "vert", "span"), P(AXES, None, None)),
        check_vma=False,
    )
```

```python
import functools

import jax
import jax.numpy as jnp
import numpy as np
from jax import lax
from jax.experimental import pallas as pl
from jax.experimental.pallas import tpu as pltpu
from jax.sharding import PartitionSpec as P

F32 = jnp.float32
UU, G2, M, ULU, T2, Q, S = range(7)
AXES = ("stream", "vert", "span")
SHARDS = P(AXES, None)
gll_inner = [
    -0.8717401485096066,
    -0.5917001814331423,
    -0.2092992179024789,
    0.2092992179024789,
    0.5917001814331423,
    0.8717401485096066,
]
MOMENTS = (((1, 2, 1.0), (2, 1, -1.0)), ((0, 2, -1.0), (2, 0, 1.0)), ((0, 1, 1.0), (1, 0, -1.0)))


def legendre_seven(points):
    before = points * 0.0 + 1.0
    current = points * 1.0
    for order in range(1, 7):
        following = ((2 * order + 1) * points * current - order * before) / (order + 1)
        before = current
        current = following
    return current


def gll_tables():
    degree = 7
    points = np.array([-1.0] + gll_inner + [1.0])
    legendre_at = legendre_seven(points)
    weights = 2.0 / (degree * (degree + 1) * legendre_at**2)
    derivative = np.zeros((8, 8))
    for i in range(8):
        for j in range(8):
            if i != j:
                derivative[i, j] = legendre_at[i] / (legendre_at[j] * (points[i] - points[j]))
    derivative[0, 0] = -degree * (degree + 1) / 4.0
    derivative[7, 7] = degree * (degree + 1) / 4.0
    return derivative, weights


DERIV, WEIGHTS = gll_tables()
STIFF = DERIV.T @ np.diag(WEIGHTS) @ DERIV


def constants():
    def f32(a):
        return np.asarray(a, np.float32)

    lane_k = f32(np.kron(np.eye(16), STIFF))
    lane_i = f32(np.kron(np.eye(2), np.kron(STIFF, np.eye(8))))
    rows = f32(np.kron(np.eye(32), STIFF))
    wj = np.tile(WEIGHTS[:, None], (1, 128))
    wk = np.tile(np.tile(WEIGHTS, 16)[None], (8, 1))
    wi = np.tile(np.tile(np.repeat(WEIGHTS, 8), 2)[None], (8, 1))
    return lane_k, lane_i, rows, f32(np.concatenate([wj, wk, wi], axis=0))


def dot(a, b):
    return lax.dot_general(
        a,
        b,
        (((1,), (0,)), ((), ())),
        precision=lax.Precision.HIGHEST,
        preferred_element_type=F32,
    )


def lane_sums(rows, first):
    n = rows.shape[0]
    sums = jnp.sum(rows, axis=1, keepdims=True)
    place = lax.broadcasted_iota(jnp.int32, (n, 128), 0) + first
    return jnp.sum(jnp.where(lane_ids(n) == place, sums, 0.0), axis=0, keepdims=True)


def row_ids():
    return lax.broadcasted_iota(jnp.int32, (8, 128), 0)


def lane_ids(rows=8):
    return lax.broadcasted_iota(jnp.int32, (rows, 128), 1)


def join_rows(below, above):
    row = row_ids()
    new_below = below + jnp.where(row == 7, pltpu.roll(above, 7, 0), 0.0)
    new_above = above + jnp.where(row == 0, pltpu.roll(below, 1, 0), 0.0)
    return new_below, new_above


def join_lanes(tile):
    lane = lane_ids()
    k = lane % 8
    left = jnp.where((k == 0) & (lane > 0), pltpu.roll(tile, 1, 1), 0.0)
    right = jnp.where((k == 7) & (lane < 127), pltpu.roll(tile, 127, 1), 0.0)
    return tile + left + right


def call(body, outs, cost=2000, space=pltpu.VMEM, out_space=pltpu.VMEM, **kwargs):
    given, taken = pl.BlockSpec(memory_space=space), pl.BlockSpec(memory_space=out_space)

    shapes = [s if isinstance(s[0], tuple) else (s, F32) for s in outs]

    def run(*args, smem=0):
        specs = [pl.BlockSpec(memory_space=pltpu.SMEM)] * smem + [given] * (len(args) - smem)
        return pl.pallas_call(
            body,
            out_shape=[jax.ShapeDtypeStruct(*s) for s in shapes],
            in_specs=specs,
            out_specs=[taken] * len(outs),
            compiler_params=pltpu.CompilerParams(vmem_limit_bytes=16 * 2**20),
            cost_estimate=pl.CostEstimate(flops=cost * 1000, bytes_accessed=200000, transcendentals=0),
            **kwargs,
        )(*args)

    return run


def stream_added(f_ref, low_ref, high_ref, geo_ref, x_ref, up_ref, down_ref):
    low, high = in_order(low_ref[...], high_ref[...], "stream", "A" in SWAPS)
    for i in range(8):
        a = f_ref[i, 0:8, :]
        b = f_ref[i, 8:16, :]
        if i == 0:
            a = a + low[0:8, :]
            b = b + low[8:16, :]
        if i == 7:
            a = a + high[0:8, :]
            b = b + high[8:16, :]
        a, b = join_rows(a, b)
        x_ref[i, 0:8, :] = a
        x_ref[i, 8:16, :] = b
        down_ref[8 * i : 8 * i + 8, :] = a
        up_ref[8 * i : 8 * i + 8, :] = b
    down_ref[64:72, :] = geo_ref[...]
    up_ref[64:72, :] = geo_ref[...]


def vert_added(x_ref, low_ref, high_ref, geo_ref, v_ref, g_ref, right_ref, left_ref, one_ref, two_ref):
    v = lax.axis_index("vert")
    has_low = jnp.where(v > 0, 1.0, 0.0)
    has_high = jnp.where(v < 7, 1.0, 0.0)
    lane = lane_ids()
    right = [jnp.zeros((8, 128), F32) for _ in range(4)]
    left = [jnp.zeros((8, 128), F32) for _ in range(4)]
    for i in range(8):
        rows = slice(8 * i, 8 * i + 8)
        low, a = join_rows(low_ref[rows, :] * has_low, x_ref[i, 0:8, :])
        b, high = join_rows(x_ref[i, 8:16, :], high_ref[rows, :] * has_high)
        for t, tile in enumerate((low, a, b, high)):
            tile = join_lanes(tile)
            v_ref[i, 8 * t : 8 * t + 8, :] = tile
            to_right = pltpu.roll(tile, (8 * i - 120) % 128, 1)
            to_left = pltpu.roll(tile, 64 + 8 * i, 1)
            right[t] = jnp.where(lane // 8 == i, to_right, right[t])
            left[t] = jnp.where(lane // 8 == 8 + i, to_left, left[t])
    for t in range(4):
        right_ref[8 * t : 8 * t + 8, :] = right[t]
        left_ref[8 * t : 8 * t + 8, :] = left[t]
    geo = geo_ref[...]
    geo_low = low_ref[64:72, :] * has_low
    geo_high = high_ref[64:72, :] * has_high
    rows = []
    for d in range(4):
        rows.append(geo_low[2 * d + 1 : 2 * d + 2, :])
        rows.append(geo[2 * d : 2 * d + 2, :])
        rows.append(geo_high[2 * d : 2 * d + 1, :])
    extended = jnp.concatenate(rows, axis=0)
    g_ref[...] = extended
    wide = lane_ids(16)
    last = jnp.broadcast_to(extended[:, 127:128], (16, 128))
    first = jnp.broadcast_to(extended[:, 0:1], (16, 128))
    right_ref[32:48, :] = jnp.where(wide < 64, last, 0.0)
    left_ref[32:48, :] = jnp.where(wide >= 64, first, 0.0)
    one_ref[...], two_ref[...] = sent_in_order(right_ref[...], left_ref[...], "span", "C" in SWAPS)


def node_rows(geo, d, t):
    return jnp.broadcast_to(geo[4 * d + t : 4 * d + t + 1, :], (8, 128))


def span_added(
    v_ref, g_ref, right_ref, left_ref, low_ref, high_ref, kk_ref, ki_ref, kr_ref, w_ref,
    v0_ref, local_ref, part_ref, top_ref, bottom_ref, maps_ref, field,
):
    lane = lane_ids()
    wj, wk, wi = w_ref[0:8, :], w_ref[8:16, :], w_ref[16:24, :]
    got = [low_ref[8 * t : 8 * t + 8, :] + high_ref[8 * t : 8 * t + 8, :] for t in range(4)]
    halo = []
    for t in range(4):
        rows = slice(8 * t, 8 * t + 8)
        from_own_first = pltpu.roll(left_ref[rows, :], 71, 1)
        from_own_last = pltpu.roll(right_ref[rows, :], 57, 1)
        tile = got[t] + jnp.where((lane < 64) & (lane % 8 == 7), from_own_first, 0.0)
        halo.append(tile + jnp.where((lane >= 64) & (lane % 8 == 0), from_own_last, 0.0))
    own = [[None] * 4 for _ in range(8)]
    for i in range(8):
        for t in range(4):
            first = pltpu.roll(got[t], (-(8 * i + 7)) % 128, 1)
            last = pltpu.roll(got[t], (63 - 8 * i) % 128, 1)
            tile = v_ref[i, 8 * t : 8 * t + 8, :]
            tile = tile + jnp.where(lane == 0, first, 0.0) + jnp.where(lane == 127, last, 0.0)
            own[i][t] = tile
            field[32 * i + 8 * t : 32 * i + 8 * t + 8, :] = tile
        v0_ref[i, 0:8, :] = own[i][1]
        v0_ref[i, 8:16, :] = own[i][2]
    for t in range(4):
        field[256 + 8 * t : 264 + 8 * t, :] = halo[t]
    along_k = dot(field[...], kk_ref[...])
    along_j = dot(kr_ref[...], field[0:256, :])
    halo_j = dot(kr_ref[0:32, 0:32], field[256:288, :])
    halo_i = dot(field[256:288, :], ki_ref[...])

    geo = g_ref[...]
    geo_halo = low_ref[32:48, :] + high_ref[32:48, :]
    out = [[None] * 4 for _ in range(8)]
    out_halo = []
    for t in range(4):
        g0, g1, g2, g3 = [node_rows(geo, d, t) for d in range(4)]
        f0, f1, f2, f3 = g0 * wj * wk, g1 * wk, g2 * wj, 50.0 * g3 * wj * wk
        if t in (1, 2):
            for d, f in enumerate((f0, f1, f2, f3)):
                maps_ref[d, 8 * t - 8 : 8 * t, :] = f
        for i in range(8):
            along_i = own[0][t] * float(STIFF[i, 0])
            for q in range(1, 8):
                along_i = along_i + own[q][t] * float(STIFF[i, q])
            at = slice(32 * i + 8 * t, 32 * i + 8 * t + 8)
            inner = f1 * along_j[at, :] + f2 * along_k[at, :] + f3 * own[i][t]
            out[i][t] = f0 * along_i + float(WEIGHTS[i]) * inner
        h0, h1, h2, h3 = [node_rows(geo_halo, d, t) for d in range(4)]
        at = slice(8 * t, 8 * t + 8)
        total = h0 * wj * wk * halo_i[at, :] + h1 * wi * wk * halo_j[at, :]
        total = total + h2 * wi * wj * along_k[256 + 8 * t : 264 + 8 * t, :]
        out_halo.append(total + 50.0 * h3 * wi * wj * wk * halo[t])

    row = row_ids()

    def middle(tiles):
        low, a, b, high = tiles
        new_a = a + jnp.where(row == 0, pltpu.roll(low, 1, 0), 0.0) + jnp.where(row == 7, pltpu.roll(b, 7, 0), 0.0)
        new_b = b + jnp.where(row == 0, pltpu.roll(a, 1, 0), 0.0) + jnp.where(row == 7, pltpu.roll(high, 7, 0), 0.0)
        return new_a, new_b

    beside = middle(out_halo)
    outer = {0: [], 7: []}
    for i in range(8):
        local_ref[i, 0:8, :] = out[i][1]
        local_ref[i, 8:16, :] = out[i][2]
        for b, tile in enumerate(middle(out[i])):
            tile = join_lanes(tile)
            first = pltpu.roll(beside[b], (-(8 * i + 7)) % 128, 1)
            last = pltpu.roll(beside[b], (63 - 8 * i) % 128, 1)
            tile = tile + jnp.where(lane == 0, first, 0.0) + jnp.where(lane == 127, last, 0.0)
            part_ref[i, 8 * b : 8 * b + 8, :] = tile
            if i in (0, 7):
                outer[i].append(tile)
    top, bottom = [jnp.concatenate(outer[i], axis=0) for i in (7, 0)]
    top_ref[...], bottom_ref[...] = sent_in_order(top, bottom, "stream", "D" in SWAPS)


def share_maps():
    s, v, w = [lax.axis_index(a) for a in AXES]
    row, lane = row_ids(), lane_ids()
    k = lane % 8
    shared = ((k == 0) & ((lane > 0) | (w > 0))) | ((k == 7) & ((lane < 127) | (w < 3)))
    span = jnp.where(shared, 0.5, 1.0)
    first = ((row == 0) & (v > 0)) | (row == 7)
    second = (row == 0) | ((row == 7) & (v < 7))
    tiles = (jnp.where(first, 0.5, 1.0) * span, jnp.where(second, 0.5, 1.0) * span)
    low = jnp.where(s > 0, 0.5, 1.0)
    high = jnp.where(s < 15, 0.5, 1.0)
    return tiles, [low] + [1.0] * 6 + [high]


def face_tiles(tiles):
    lane, row = lane_ids(), row_ids()
    out = []
    for side in range(2):
        out += [tiles[7 * side][0], tiles[7 * side][1]]
    for side in range(2):
        for b in range(2):
            tile = jnp.zeros((8, 128), F32)
            for i in range(8):
                tile = jnp.where(row == i, pltpu.roll(tiles[i][b], (i - 7 * side) % 8, 0), tile)
            out.append(tile)
    for side in range(2):
        for b in range(2):
            tile = jnp.zeros((8, 128), F32)
            for i in range(8):
                tile = jnp.where(lane % 8 == i, pltpu.roll(tiles[i][b], (i - 7 * side) % 128, 1), tile)
            out.append(tile)
    return [tile if (n // 2) % 2 == 0 else -tile for n, tile in enumerate(out)]


def load_rows(faces, omega_ref):
    sums = [[None] * 4 for _ in range(6)]
    for d in range(3):
        targets = [(d, 1.0)] + [(3 + c, sign) for c, _, sign in MOMENTS[d]]
        for q, (component, sign) in enumerate(targets):
            for store in range(4):
                total = None
                for face in (2 * d, 2 * d + 1):
                    for b in range(2):
                        term = omega_ref[((2 * face + b) * 5 + store) * 3 + q] * faces[2 * face + b]
                        total = term if total is None else total + term
                total = total * sign
                before = sums[component][store]
                sums[component][store] = total if before is None else before + total
    return [jnp.sum(sums[c][s], axis=0, keepdims=True) for c in range(6) for s in range(4)]


def zero_rows(n):
    return [jnp.zeros((n, 128), F32)]


def sublane_sum(tile):
    return jnp.sum(tile, axis=0, keepdims=True)


def before_image(v0_ref, local_ref, part_ref, omega_ref, pre_ref):
    share, layers = share_maps()
    norm = energy = top = bottom = jnp.zeros((8, 128), F32)
    tiles = [[v0_ref[i, 0:8, :], v0_ref[i, 8:16, :]] for i in range(8)]
    for i in range(8):
        for b in range(2):
            x = tiles[i][b]
            square = x * x * share[b]
            norm = norm + square * layers[i]
            energy = energy + x * local_ref[i, 8 * b : 8 * b + 8, :]
            if 0 < i < 7:
                bottom = bottom + square
                top = top + x * part_ref[i, 8 * b : 8 * b + 8, :] * share[b]
    rows = [sublane_sum(top), sublane_sum(norm), sublane_sum(bottom)] + zero_rows(1)
    rows += [sublane_sum(energy)] + zero_rows(3) + load_rows(face_tiles(tiles), omega_ref)
    sums = lane_sums(jnp.concatenate(rows, axis=0), 0)
    lane = lane_ids(1)
    over, norm, under, energy = sums[:, 0:1], sums[:, 1:2], sums[:, 2:3], sums[:, 4:5]
    usable = under > 1e-30
    quotient = jnp.where(usable, over / jnp.where(usable, under, 1.0), 0.0)
    quotient = jnp.clip(quotient, 0.0, 1e6)
    row = jnp.where(lane >= 8, sums, 0.0)
    for n, value in ((M, norm), (Q, energy), (S, quotient)):
        row = jnp.where(lane == n, value, row)
    pre_ref[...] = jnp.broadcast_to(row, (8, 128))


def image_sums(
    v0_ref, local_ref, part_ref, low_ref, high_ref, maps_ref, omega_ref, pre_ref, kk_ref, kr_ref,
    v1_ref, out_ref, field,
):
    share, layers = share_maps()
    low, high = in_order(low_ref[...], high_ref[...], "stream", "D" in SWAPS)
    quotient = jnp.broadcast_to(pre_ref[:, S : S + 1], (8, 128))
    v1 = [[None] * 2 for _ in range(8)]
    u = [[None] * 2 for _ in range(8)]
    norm = cross_norm = energy = cross_energy = jnp.zeros((8, 128), F32)
    for i in range(8):
        for b in range(2):
            rows = slice(8 * b, 8 * b + 8)
            tile = part_ref[i, rows, :]
            if i == 0:
                tile = tile + low[rows, :]
            if i == 7:
                tile = tile + high[rows, :]
            v1[i][b] = tile
            v1_ref[i, rows, :] = tile
            x = v0_ref[i, rows, :]
            y = tile - quotient * x
            u[i][b] = y
            field[16 * i + 8 * b : 16 * i + 8 * b + 8, :] = y
            weighted = y * share[b] * layers[i]
            norm = norm + y * weighted
            cross_norm = cross_norm + x * weighted
            cross_energy = cross_energy + y * local_ref[i, rows, :]
    along_k = dot(field[...], kk_ref[...])
    along_j = dot(kr_ref[0:128, 0:128], field[...])
    for b in range(2):
        rows = slice(8 * b, 8 * b + 8)
        f0, f1, f2, f3 = [maps_ref[d, rows, :] for d in range(4)]
        for i in range(8):
            along_i = u[0][b] * float(STIFF[i, 0])
            for q in range(1, 8):
                along_i = along_i + u[q][b] * float(STIFF[i, q])
            at = slice(16 * i + 8 * b, 16 * i + 8 * b + 8)
            inner = f1 * along_j[at, :] + f2 * along_k[at, :] + f3 * u[i][b]
            energy = energy + u[i][b] * (f0 * along_i + float(WEIGHTS[i]) * inner)
    rows = [sublane_sum(a) for a in (norm, 2.0 * cross_norm)] + zero_rows(1)
    rows += [sublane_sum(a) for a in (energy, 2.0 * cross_energy)] + zero_rows(3)
    row = lane_sums(jnp.concatenate(rows, axis=0), 0)
    row = row + lane_sums(jnp.concatenate(load_rows(face_tiles(v1), omega_ref), axis=0), 32)
    out_ref[...] = jnp.broadcast_to(row + pre_ref[0:1, :], out_ref.shape)


def merged(parts):
    n = parts.shape[0]
    lane = lane_ids(n)
    common = parts[0:1, S : S + 1]
    e = parts[:, S : S + 1] - common
    once = jnp.where((lane == UU) | (lane == ULU), 1.0, jnp.where((lane == G2) | (lane == T2), 2.0, 0.0))
    twice = jnp.where((lane == UU) | (lane == ULU), 1.0, 0.0)
    rows = parts + e * (once * pltpu.roll(parts, 127, 1) + e * (twice * pltpu.roll(parts, 126, 1)))
    total = jnp.sum(rows, axis=0, keepdims=True)
    return jnp.where(lane_ids(1) == S, common, total)


def group_sums(parts_ref, out_ref):
    out_ref[...] = jnp.broadcast_to(merged(parts_ref[...]), out_ref.shape)


def finish(
    parts_ref, v0_ref, v1_ref, arm_ref, store_ref, motion_ref, p_out, velocity_out, p_ref, velocity_ref, sems
):
    total = merged(parts_ref[...])
    uu, g2, m, ulu, t2, q, s = [total[:, n : n + 1] for n in range(7)]
    alpha = m / q
    e = s - q / m
    uu = uu + e * (g2 + e * m)
    ulu = ulu + e * (t2 + e * q)
    square = alpha * alpha
    beta = square * uu / m
    curve = square * ulu - beta * beta * q
    alpha_next = square * uu / curve
    c0 = alpha + alpha_next * (1.0 + beta)
    c1 = -alpha_next * alpha
    wide0 = jnp.broadcast_to(c0, (16, 128))
    wide1 = jnp.broadcast_to(c1, (16, 128))
    for i in range(8):
        p_ref[i] = wide0 * v0_ref[i] + wide1 * v1_ref[i]
    p_copy = pltpu.make_async_copy(p_ref, p_out, sems.at[0])
    p_copy.start()
    loads = c0 * total + c1 * pltpu.roll(total, 104, 1)
    state = motion_ref[0:1, :] + motion_ref[1:2, :] * loads
    stores = store_ref[...]
    maps = []
    for c in range(6):
        value = jnp.zeros((32, 128), F32)
        for store in range(4):
            at = 8 + 4 * c + store
            value = jnp.where(stores == store, state[:, at : at + 1], value)
        maps.append(value)
    arms = [arm_ref[c] for c in range(3)]
    for c in range(3):
        a, b = (c + 1) % 3, (c + 2) % 3
        velocity_ref[c] = maps[c] + (maps[3 + a] * arms[b] - maps[3 + b] * arms[a])
    velocity_copy = pltpu.make_async_copy(velocity_ref, velocity_out, sems.at[1])
    velocity_copy.start()
    p_copy.wait()
    velocity_copy.wait()


def spread_geometry(geo_ref, out_ref):
    element = lax.broadcasted_iota(jnp.int32, (16, 128), 0)
    out_ref[...] = dot(geo_ref[...], jnp.where((lane_ids(16) >> 3) == element, 1.0, 0.0))


def wall_table(
    elem_ref, face_ref, stores_ref, motion_ref, inverse_ref, weight_ref, arm_ref,
    table_ref, code_ref, store_out, motion_out,
):
    weight = weight_ref[...]
    nodes = jnp.concatenate([weight] + [weight * arm_ref[c] for c in range(3)], axis=0)
    a = lax.broadcasted_iota(jnp.int32, (128, 128), 0)
    b = lax.broadcasted_iota(jnp.int32, (128, 128), 1)
    slot, outer, inner = a & 64, (a >> 3) & 7, a & 7
    table_ref[0:128, :] = dot(nodes, jnp.where(b == slot + (7 - outer) * 8 + inner, 1.0, 0.0))
    table_ref[128:256, :] = dot(nodes, jnp.where(b == slot + (7 - inner) * 8 + outer, 1.0, 0.0))

    elem, face, stores = elem_ref[...], face_ref[...], stores_ref[...]
    n = lax.broadcasted_iota(jnp.int32, (1, 64), 1)
    direction = face >> 1
    first = jnp.where(direction == 2, 128, 0) + (n >> 1)
    column = elem & 15
    code_ref[0:1, :] = ((2 * face + (elem >> 4)) * 5 + stores) * 3
    code_ref[1:2, :] = column
    code_ref[2:3, :] = (8 * column + 64 * (n & 1) + 72) & 127
    code_ref[3:4, :] = first
    code_ref[4:5, :] = first + jnp.where(direction == 2, 64, 96)
    code_ref[5:6, :] = first + jnp.where(direction == 0, 64, 32)
    code_ref[6:8, :] = jnp.zeros((2, 64), jnp.int32)

    numbers = stores.astype(F32)
    row = lax.broadcasted_iota(jnp.int32, (32, 64), 0)
    column = lax.broadcasted_iota(jnp.int32, (32, 64), 1)
    even = jnp.sum(jnp.where(column == 2 * row, numbers, 0.0), axis=1, keepdims=True)
    odd = jnp.sum(jnp.where(column == 2 * row + 1, numbers, 0.0), axis=1, keepdims=True)
    store_out[...] = jnp.where(lane_ids(32) < 64, even, odd)

    load = lane_ids(8) - 8
    inside = (load >= 0) & (load < 24)
    component, store = load >> 2, load & 3
    row = row_ids()
    motion = dot(motion_ref[...], jnp.where(inside & (component == row), 1.0, 0.0)[0:6, :])
    motion_out[0:1, :] = jnp.sum(jnp.where((store == row)[0:4, :], motion, 0.0), axis=0, keepdims=True)
    scale = dot(inverse_ref[...], jnp.where(inside & (store == row), 1.0, 0.0)[0:4, :])
    taken = jnp.maximum(component - 2, 0) == row
    motion_out[1:2, :] = jnp.sum(jnp.where(taken[0:4, :], scale, 0.0), axis=0, keepdims=True)


def wall_weights(begin, end, code_ref, table_ref, *rest):
    omega_ref = rest[-1]
    if begin == 0:
        omega_ref[...] = jnp.zeros(omega_ref.shape, F32)
    lane = lane_ids() >> 3

    def add(step, carry):
        tiles = []
        for k in range(8):
            n = begin + 8 * step + k
            here = lane == code_ref[1, n]
            for q in range(3):
                nodes = jnp.broadcast_to(table_ref[pl.ds(code_ref[3 + q, n], 1), :], (8, 128))
                nodes = pltpu.roll(pltpu.roll(nodes, 0, 1, stride=8, stride_axis=0), code_ref[2, n], 1)
                tiles.append(jnp.where(here, nodes, 0.0))
        for k in range(8):
            at = code_ref[0, begin + 8 * step + k]
            for q in range(3):
                omega_ref[at + q] += tiles[3 * k + q]
        return carry

    lax.fori_loop(0, (end - begin) // 8, add, 0)


def shifted(x, axis, step, ring=False):
    count = lax.axis_size(axis)
    pairs = [(i, (i + step) % count) for i in range(count) if ring or 0 <= i + step < count]
    return lax.ppermute(x, axis, pairs)


def swapped(x, axis, first):
    pairs = [(i, i + 1) for i in range(first, lax.axis_size(axis) - 1, 2)]
    return lax.ppermute(x, axis, pairs + [(b, a) for a, b in pairs])


SWAPS = "AC"
HEAD = 8
LEAD = 22
FIRST = 32
SPLIT = 32


def reduced(sums):
    for axes, count, first in ((("vert", "span"), 32, LEAD), ("stream", 16, HEAD)):
        lists = [[(first + n) % count for n in range(count)]]
        sums = lax.all_to_all(sums.reshape(count, 1, 128), axes, 0, 0, axis_index_groups=lists).reshape(count, 128)
        if count == 32:
            sums = call(group_sums, [(16, 128)])(sums)[0]
    return sums


def exchange(one, two, axis, swap):
    if swap:
        later = swapped(two, axis, 1)
        return swapped(one, axis, 0), later
    return shifted(one, axis, 1), shifted(two, axis, -1)


def in_order(first, second, axis, swap):
    if not swap:
        return first, second
    even = lax.axis_index(axis) % 2 == 0
    return jnp.where(even, second, first), jnp.where(even, first, second)


def sent_in_order(up, down, axis, swap):
    if not swap:
        return up, down
    even = lax.axis_index(axis) % 2 == 0
    return jnp.where(even, up, down), jnp.where(even, down, up)


def per_device(
    forcing, geometry, wall_elem, wall_face, wall_store, wall_weight, wall_arm, store_motion, store_inverse
):
    lane_k, lane_i, rows, node_w = [jnp.asarray(a) for a in constants()]
    field = (8, 16, 128)
    tie = lax.optimization_barrier

    if "A" in SWAPS:
        odd = lax.axis_index("stream") % 2
        top, bottom = [lax.dynamic_index_in_dim(forcing, at, 0, False) for at in (7 - 7 * odd, 7 * odd)]
    else:
        top, bottom = forcing[7], forcing[0]
    low, high = exchange(top, bottom, "stream", "A" in SWAPS)
    geo = call(spread_geometry, [(8, 128)])(geometry.reshape(8, 16))[0]
    x, up, down = call(stream_added, [field, (72, 128), (72, 128)])(forcing, low, high, geo)

    up, down, weight, arms = tie((up, down, wall_weight.reshape(32, 128), wall_arm.reshape(3, 32, 128)))
    low = shifted(up, "vert", 1, ring=True)
    high = shifted(down, "vert", -1, ring=True)
    table, codes, store_rows, motion = call(
        wall_table, [(256, 128), ((8, 64), jnp.int32), (32, 128), (2, 128)]
    )(wall_elem, wall_face, wall_store, store_motion.T, store_inverse, weight, arms)
    omega = call(functools.partial(wall_weights, 0, SPLIT), [(180, 8, 128)])(codes, table, smem=1)[0]
    low, high, table, codes, omega = tie((low, high, table, codes, omega))
    wide, geo_wide, right, left, to_one, to_two = call(vert_added, [(8, 32, 128), (16, 128)] + [(48, 128)] * 4)(
        x, low, high, geo
    )

    to_one, to_two, table, codes, omega = tie((to_one, to_two, table, codes, omega))
    low, high = exchange(to_one, to_two, "span", "C" in SWAPS)
    omega = call(functools.partial(wall_weights, SPLIT, 64), [(180, 8, 128)], input_output_aliases={2: 0})(
        codes, table, omega, smem=1
    )[0]
    low, high, omega = tie((low, high, omega))
    v0, local, part, top, bottom, maps = call(
        span_added,
        [field, field, field, (16, 128), (16, 128), (4, 16, 128)],
        scratch_shapes=[pltpu.VMEM((288, 128), F32)],
    )(wide, geo_wide, right, left, low, high, lane_k, lane_i, rows, node_w)

    low, high = exchange(top, bottom, "stream", "D" in SWAPS)
    pre = call(before_image, [(8, 128)])(v0, local, part, omega)[0]
    v1, sums = call(image_sums, [field, (FIRST, 128)], scratch_shapes=[pltpu.VMEM((128, 128), F32)])(
        v0, local, part, low, high, maps, omega, pre, lane_k, rows
    )
    sums = reduced(sums)
    pressure, velocity = call(
        finish,
        [field, (3, 32, 128)],
        out_space=pltpu.HBM,
        scratch_shapes=[pltpu.VMEM(field, F32), pltpu.VMEM((3, 32, 128), F32), pltpu.SemaphoreType.DMA((2,))],
    )(sums, v0, v1, arms, store_rows, motion)
    return pressure, velocity.reshape(1, 3, 4096)


def solution(mesh):
    return jax.shard_map(
        per_device,
        mesh=mesh,
        in_specs=(
            P("stream", "vert", "span"),
            P(None, "stream", "vert", "span"),
            SHARDS,
            SHARDS,
            SHARDS,
            SHARDS,
            P(AXES, None, None),
            P(),
            P(),
        ),
        out_specs=(P("stream", "vert", "span"), P(AXES, None, None)),
        check_vma=False,
    )
```

```python
import functools

import jax
import jax.numpy as jnp
import numpy as np
from jax import lax
from jax.experimental import pallas as pl
from jax.experimental.pallas import tpu as pltpu
from jax.sharding import PartitionSpec as P

F32 = jnp.float32
UU, G2, M, ULU, T2, Q, S = range(7)
AXES = ("stream", "vert", "span")
SHARDS = P(AXES, None)
gll_inner = [
    -0.8717401485096066,
    -0.5917001814331423,
    -0.2092992179024789,
    0.2092992179024789,
    0.5917001814331423,
    0.8717401485096066,
]
MOMENTS = (((1, 2, 1.0), (2, 1, -1.0)), ((0, 2, -1.0), (2, 0, 1.0)), ((0, 1, 1.0), (1, 0, -1.0)))


def legendre_seven(points):
    before = points * 0.0 + 1.0
    current = points * 1.0
    for order in range(1, 7):
        following = ((2 * order + 1) * points * current - order * before) / (order + 1)
        before = current
        current = following
    return current


def gll_tables():
    degree = 7
    points = np.array([-1.0] + gll_inner + [1.0])
    legendre_at = legendre_seven(points)
    weights = 2.0 / (degree * (degree + 1) * legendre_at**2)
    derivative = np.zeros((8, 8))
    for i in range(8):
        for j in range(8):
            if i != j:
                derivative[i, j] = legendre_at[i] / (legendre_at[j] * (points[i] - points[j]))
    derivative[0, 0] = -degree * (degree + 1) / 4.0
    derivative[7, 7] = degree * (degree + 1) / 4.0
    return derivative, weights


DERIV, WEIGHTS = gll_tables()
STIFF = DERIV.T @ np.diag(WEIGHTS) @ DERIV


def constants():
    def f32(a):
        return np.asarray(a, np.float32)

    lane_k = f32(np.kron(np.eye(16), STIFF))
    lane_i = f32(np.kron(np.eye(2), np.kron(STIFF, np.eye(8))))
    rows = f32(np.kron(np.eye(32), STIFF))
    wj = np.tile(WEIGHTS[:, None], (1, 128))
    wk = np.tile(np.tile(WEIGHTS, 16)[None], (8, 1))
    wi = np.tile(np.tile(np.repeat(WEIGHTS, 8), 2)[None], (8, 1))
    return lane_k, lane_i, rows, f32(np.concatenate([wj, wk, wi], axis=0))


def dot(a, b):
    return lax.dot_general(
        a,
        b,
        (((1,), (0,)), ((), ())),
        precision=lax.Precision.HIGHEST,
        preferred_element_type=F32,
    )


def lane_sums(rows, first):
    n = rows.shape[0]
    sums = jnp.sum(rows, axis=1, keepdims=True)
    place = lax.broadcasted_iota(jnp.int32, (n, 128), 0) + first
    return jnp.sum(jnp.where(lane_ids(n) == place, sums, 0.0), axis=0, keepdims=True)


def row_ids():
    return lax.broadcasted_iota(jnp.int32, (8, 128), 0)


def lane_ids(rows=8):
    return lax.broadcasted_iota(jnp.int32, (rows, 128), 1)


def join_rows(below, above):
    row = row_ids()
    new_below = below + jnp.where(row == 7, pltpu.roll(above, 7, 0), 0.0)
    new_above = above + jnp.where(row == 0, pltpu.roll(below, 1, 0), 0.0)
    return new_below, new_above


def join_lanes(tile):
    lane = lane_ids()
    k = lane % 8
    left = jnp.where((k == 0) & (lane > 0), pltpu.roll(tile, 1, 1), 0.0)
    right = jnp.where((k == 7) & (lane < 127), pltpu.roll(tile, 127, 1), 0.0)
    return tile + left + right


def call(body, outs, cost=2000, space=pltpu.VMEM, out_space=pltpu.VMEM, **kwargs):
    given, taken = pl.BlockSpec(memory_space=space), pl.BlockSpec(memory_space=out_space)

    shapes = [s if isinstance(s[0], tuple) else (s, F32) for s in outs]

    def run(*args, smem=0):
        specs = [pl.BlockSpec(memory_space=pltpu.SMEM)] * smem + [given] * (len(args) - smem)
        return pl.pallas_call(
            body,
            out_shape=[jax.ShapeDtypeStruct(*s) for s in shapes],
            in_specs=specs,
            out_specs=[taken] * len(outs),
            compiler_params=pltpu.CompilerParams(vmem_limit_bytes=16 * 2**20),
            cost_estimate=pl.CostEstimate(flops=cost * 1000, bytes_accessed=200000, transcendentals=0),
            **kwargs,
        )(*args)

    return run


def stream_added(f_ref, low_ref, high_ref, geo_ref, x_ref, up_ref, down_ref):
    low, high = in_order(low_ref[...], high_ref[...], "A")
    for i in range(8):
        a = f_ref[i, 0:8, :]
        b = f_ref[i, 8:16, :]
        if i == 0:
            a = a + low[0:8, :]
            b = b + low[8:16, :]
        if i == 7:
            a = a + high[0:8, :]
            b = b + high[8:16, :]
        a, b = join_rows(a, b)
        x_ref[i, 0:8, :] = a
        x_ref[i, 8:16, :] = b
        one, two = sent_in_order(b, a, "B")
        up_ref[8 * i : 8 * i + 8, :] = one
        down_ref[8 * i : 8 * i + 8, :] = two
    down_ref[64:72, :] = geo_ref[...]
    up_ref[64:72, :] = geo_ref[...]


def vert_added(x_ref, low_ref, high_ref, geo_ref, v_ref, g_ref, right_ref, left_ref, one_ref, two_ref):
    v = lax.axis_index("vert")
    has_low = jnp.where(v > 0, 1.0, 0.0)
    has_high = jnp.where(v < 7, 1.0, 0.0)
    lane = lane_ids()
    right = [jnp.zeros((8, 128), F32) for _ in range(4)]
    left = [jnp.zeros((8, 128), F32) for _ in range(4)]
    for i in range(8):
        rows = slice(8 * i, 8 * i + 8)
        low, high = in_order(low_ref[rows, :], high_ref[rows, :], "B")
        low, a = join_rows(low * has_low, x_ref[i, 0:8, :])
        b, high = join_rows(x_ref[i, 8:16, :], high * has_high)
        for t, tile in enumerate((low, a, b, high)):
            tile = join_lanes(tile)
            v_ref[i, 8 * t : 8 * t + 8, :] = tile
            to_right = pltpu.roll(tile, (8 * i - 120) % 128, 1)
            to_left = pltpu.roll(tile, 64 + 8 * i, 1)
            right[t] = jnp.where(lane // 8 == i, to_right, right[t])
            left[t] = jnp.where(lane // 8 == 8 + i, to_left, left[t])
    for t in range(4):
        right_ref[8 * t : 8 * t + 8, :] = right[t]
        left_ref[8 * t : 8 * t + 8, :] = left[t]
    geo = geo_ref[...]
    geo_low, geo_high = in_order(low_ref[64:72, :], high_ref[64:72, :], "B")
    geo_low, geo_high = geo_low * has_low, geo_high * has_high
    rows = []
    for d in range(4):
        rows.append(geo_low[2 * d + 1 : 2 * d + 2, :])
        rows.append(geo[2 * d : 2 * d + 2, :])
        rows.append(geo_high[2 * d : 2 * d + 1, :])
    extended = jnp.concatenate(rows, axis=0)
    g_ref[...] = extended
    wide = lane_ids(16)
    last = jnp.broadcast_to(extended[:, 127:128], (16, 128))
    first = jnp.broadcast_to(extended[:, 0:1], (16, 128))
    right_ref[32:48, :] = jnp.where(wide < 64, last, 0.0)
    left_ref[32:48, :] = jnp.where(wide >= 64, first, 0.0)
    one_ref[...], two_ref[...] = sent_in_order(right_ref[...], left_ref[...], "C")


def node_rows(geo, d, t):
    return jnp.broadcast_to(geo[4 * d + t : 4 * d + t + 1, :], (8, 128))


def span_added(
    v_ref, g_ref, right_ref, left_ref, low_ref, high_ref, kk_ref, ki_ref, kr_ref, w_ref,
    v0_ref, local_ref, part_ref, top_ref, bottom_ref, maps_ref, field,
):
    lane = lane_ids()
    wj, wk, wi = w_ref[0:8, :], w_ref[8:16, :], w_ref[16:24, :]
    got = [low_ref[8 * t : 8 * t + 8, :] + high_ref[8 * t : 8 * t + 8, :] for t in range(4)]
    halo = []
    for t in range(4):
        rows = slice(8 * t, 8 * t + 8)
        from_own_first = pltpu.roll(left_ref[rows, :], 71, 1)
        from_own_last = pltpu.roll(right_ref[rows, :], 57, 1)
        tile = got[t] + jnp.where((lane < 64) & (lane % 8 == 7), from_own_first, 0.0)
        halo.append(tile + jnp.where((lane >= 64) & (lane % 8 == 0), from_own_last, 0.0))
    own = [[None] * 4 for _ in range(8)]
    for i in range(8):
        for t in range(4):
            first = pltpu.roll(got[t], (-(8 * i + 7)) % 128, 1)
            last = pltpu.roll(got[t], (63 - 8 * i) % 128, 1)
            tile = v_ref[i, 8 * t : 8 * t + 8, :]
            tile = tile + jnp.where(lane == 0, first, 0.0) + jnp.where(lane == 127, last, 0.0)
            own[i][t] = tile
            field[32 * i + 8 * t : 32 * i + 8 * t + 8, :] = tile
        v0_ref[i, 0:8, :] = own[i][1]
        v0_ref[i, 8:16, :] = own[i][2]
    for t in range(4):
        field[256 + 8 * t : 264 + 8 * t, :] = halo[t]
    along_k = dot(field[...], kk_ref[...])
    along_j = dot(kr_ref[...], field[0:256, :])
    halo_j = dot(kr_ref[0:32, 0:32], field[256:288, :])
    halo_i = dot(field[256:288, :], ki_ref[...])

    geo = g_ref[...]
    geo_halo = low_ref[32:48, :] + high_ref[32:48, :]
    out = [[None] * 4 for _ in range(8)]
    out_halo = []
    for t in range(4):
        g0, g1, g2, g3 = [node_rows(geo, d, t) for d in range(4)]
        f0, f1, f2, f3 = g0 * wj * wk, g1 * wk, g2 * wj, 50.0 * g3 * wj * wk
        if t in (1, 2):
            for d, f in enumerate((f0, f1, f2, f3)):
                maps_ref[d, 8 * t - 8 : 8 * t, :] = f
        for i in range(8):
            along_i = own[0][t] * float(STIFF[i, 0])
            for q in range(1, 8):
                along_i = along_i + own[q][t] * float(STIFF[i, q])
            at = slice(32 * i + 8 * t, 32 * i + 8 * t + 8)
            inner = f1 * along_j[at, :] + f2 * along_k[at, :] + f3 * own[i][t]
            out[i][t] = f0 * along_i + float(WEIGHTS[i]) * inner
        h0, h1, h2, h3 = [node_rows(geo_halo, d, t) for d in range(4)]
        at = slice(8 * t, 8 * t + 8)
        total = h0 * wj * wk * halo_i[at, :] + h1 * wi * wk * halo_j[at, :]
        total = total + h2 * wi * wj * along_k[256 + 8 * t : 264 + 8 * t, :]
        out_halo.append(total + 50.0 * h3 * wi * wj * wk * halo[t])

    row = row_ids()

    def middle(tiles):
        low, a, b, high = tiles
        new_a = a + jnp.where(row == 0, pltpu.roll(low, 1, 0), 0.0) + jnp.where(row == 7, pltpu.roll(b, 7, 0), 0.0)
        new_b = b + jnp.where(row == 0, pltpu.roll(a, 1, 0), 0.0) + jnp.where(row == 7, pltpu.roll(high, 7, 0), 0.0)
        return new_a, new_b

    beside = middle(out_halo)
    outer = {0: [], 7: []}
    for i in range(8):
        local_ref[i, 0:8, :] = out[i][1]
        local_ref[i, 8:16, :] = out[i][2]
        for b, tile in enumerate(middle(out[i])):
            tile = join_lanes(tile)
            first = pltpu.roll(beside[b], (-(8 * i + 7)) % 128, 1)
            last = pltpu.roll(beside[b], (63 - 8 * i) % 128, 1)
            tile = tile + jnp.where(lane == 0, first, 0.0) + jnp.where(lane == 127, last, 0.0)
            part_ref[i, 8 * b : 8 * b + 8, :] = tile
            if i in (0, 7):
                outer[i].append(tile)
    top, bottom = [jnp.concatenate(outer[i], axis=0) for i in (7, 0)]
    top_ref[...], bottom_ref[...] = sent_in_order(top, bottom, "D")


def share_maps():
    s, v, w = [lax.axis_index(a) for a in AXES]
    row, lane = row_ids(), lane_ids()
    k = lane % 8
    shared = ((k == 0) & ((lane > 0) | (w > 0))) | ((k == 7) & ((lane < 127) | (w < 3)))
    span = jnp.where(shared, 0.5, 1.0)
    first = ((row == 0) & (v > 0)) | (row == 7)
    second = (row == 0) | ((row == 7) & (v < 7))
    tiles = (jnp.where(first, 0.5, 1.0) * span, jnp.where(second, 0.5, 1.0) * span)
    low = jnp.where(s > 0, 0.5, 1.0)
    high = jnp.where(s < 15, 0.5, 1.0)
    return tiles, [low] + [1.0] * 6 + [high]


def face_tiles(tiles):
    lane, row = lane_ids(), row_ids()
    out = []
    for side in range(2):
        out += [tiles[7 * side][0], tiles[7 * side][1]]
    for side in range(2):
        for b in range(2):
            tile = jnp.zeros((8, 128), F32)
            for i in range(8):
                tile = jnp.where(row == i, pltpu.roll(tiles[i][b], (i - 7 * side) % 8, 0), tile)
            out.append(tile)
    for side in range(2):
        for b in range(2):
            tile = jnp.zeros((8, 128), F32)
            for i in range(8):
                tile = jnp.where(lane % 8 == i, pltpu.roll(tiles[i][b], (i - 7 * side) % 128, 1), tile)
            out.append(tile)
    return [tile if (n // 2) % 2 == 0 else -tile for n, tile in enumerate(out)]


def load_rows(faces, omega_ref):
    sums = [[None] * 4 for _ in range(6)]
    for d in range(3):
        targets = [(d, 1.0)] + [(3 + c, sign) for c, _, sign in MOMENTS[d]]
        for q, (component, sign) in enumerate(targets):
            for store in range(4):
                total = None
                for face in (2 * d, 2 * d + 1):
                    for b in range(2):
                        term = omega_ref[((2 * face + b) * 5 + store) * 3 + q] * faces[2 * face + b]
                        total = term if total is None else total + term
                total = total * sign
                before = sums[component][store]
                sums[component][store] = total if before is None else before + total
    return [jnp.sum(sums[c][s], axis=0, keepdims=True) for c in range(6) for s in range(4)]


def zero_rows(n):
    return [jnp.zeros((n, 128), F32)]


def sublane_sum(tile):
    return jnp.sum(tile, axis=0, keepdims=True)


def before_image(v0_ref, local_ref, part_ref, omega_ref, pre_ref):
    share, layers = share_maps()
    norm = energy = top = bottom = jnp.zeros((8, 128), F32)
    tiles = [[v0_ref[i, 0:8, :], v0_ref[i, 8:16, :]] for i in range(8)]
    for i in range(8):
        for b in range(2):
            x = tiles[i][b]
            square = x * x * share[b]
            norm = norm + square * layers[i]
            energy = energy + x * local_ref[i, 8 * b : 8 * b + 8, :]
            if 0 < i < 7:
                bottom = bottom + square
                top = top + x * part_ref[i, 8 * b : 8 * b + 8, :] * share[b]
    rows = [sublane_sum(top), sublane_sum(norm), sublane_sum(bottom)] + zero_rows(1)
    rows += [sublane_sum(energy)] + zero_rows(3) + load_rows(face_tiles(tiles), omega_ref)
    sums = lane_sums(jnp.concatenate(rows, axis=0), 0)
    lane = lane_ids(1)
    over, norm, under, energy = sums[:, 0:1], sums[:, 1:2], sums[:, 2:3], sums[:, 4:5]
    usable = under > 1e-30
    quotient = jnp.where(usable, over / jnp.where(usable, under, 1.0), 0.0)
    quotient = jnp.clip(quotient, 0.0, 1e6)
    row = jnp.where(lane >= 8, sums, 0.0)
    for n, value in ((M, norm), (Q, energy), (S, quotient)):
        row = jnp.where(lane == n, value, row)
    pre_ref[...] = jnp.broadcast_to(row, (8, 128))


def image_sums(
    v0_ref, local_ref, part_ref, low_ref, high_ref, maps_ref, omega_ref, pre_ref, kk_ref, kr_ref,
    v1_ref, out_ref, field,
):
    share, layers = share_maps()
    low, high = in_order(low_ref[...], high_ref[...], "D")
    quotient = jnp.broadcast_to(pre_ref[:, S : S + 1], (8, 128))
    v1 = [[None] * 2 for _ in range(8)]
    u = [[None] * 2 for _ in range(8)]
    norm = cross_norm = energy = cross_energy = jnp.zeros((8, 128), F32)
    for i in range(8):
        for b in range(2):
            rows = slice(8 * b, 8 * b + 8)
            tile = part_ref[i, rows, :]
            if i == 0:
                tile = tile + low[rows, :]
            if i == 7:
                tile = tile + high[rows, :]
            v1[i][b] = tile
            v1_ref[i, rows, :] = tile
            x = v0_ref[i, rows, :]
            y = tile - quotient * x
            u[i][b] = y
            field[16 * i + 8 * b : 16 * i + 8 * b + 8, :] = y
            weighted = y * share[b] * layers[i]
            norm = norm + y * weighted
            cross_norm = cross_norm + x * weighted
            cross_energy = cross_energy + y * local_ref[i, rows, :]
    along_k = dot(field[...], kk_ref[...])
    along_j = dot(kr_ref[0:128, 0:128], field[...])
    for b in range(2):
        rows = slice(8 * b, 8 * b + 8)
        f0, f1, f2, f3 = [maps_ref[d, rows, :] for d in range(4)]
        for i in range(8):
            along_i = u[0][b] * float(STIFF[i, 0])
            for q in range(1, 8):
                along_i = along_i + u[q][b] * float(STIFF[i, q])
            at = slice(16 * i + 8 * b, 16 * i + 8 * b + 8)
            inner = f1 * along_j[at, :] + f2 * along_k[at, :] + f3 * u[i][b]
            energy = energy + u[i][b] * (f0 * along_i + float(WEIGHTS[i]) * inner)
    rows = [sublane_sum(a) for a in (norm, 2.0 * cross_norm)] + zero_rows(1)
    rows += [sublane_sum(a) for a in (energy, 2.0 * cross_energy)] + zero_rows(3)
    row = lane_sums(jnp.concatenate(rows, axis=0), 0)
    row = row + lane_sums(jnp.concatenate(load_rows(face_tiles(v1), omega_ref), axis=0), 32)
    out_ref[...] = jnp.broadcast_to(row + pre_ref[0:1, :], out_ref.shape)


def merged(parts):
    n = parts.shape[0]
    lane = lane_ids(n)
    common = parts[0:1, S : S + 1]
    e = parts[:, S : S + 1] - common
    once = jnp.where((lane == UU) | (lane == ULU), 1.0, jnp.where((lane == G2) | (lane == T2), 2.0, 0.0))
    twice = jnp.where((lane == UU) | (lane == ULU), 1.0, 0.0)
    rows = parts + e * (once * pltpu.roll(parts, 127, 1) + e * (twice * pltpu.roll(parts, 126, 1)))
    total = jnp.sum(rows, axis=0, keepdims=True)
    return jnp.where(lane_ids(1) == S, common, total)


def group_sums(parts_ref, out_ref):
    out_ref[...] = jnp.broadcast_to(merged(parts_ref[...]), out_ref.shape)


def finish(
    parts_ref, v0_ref, v1_ref, arm_ref, store_ref, motion_ref, p_out, velocity_out, p_ref, velocity_ref, sems
):
    total = merged(parts_ref[...])
    uu, g2, m, ulu, t2, q, s = [total[:, n : n + 1] for n in range(7)]
    alpha = m / q
    e = s - q / m
    uu = uu + e * (g2 + e * m)
    ulu = ulu + e * (t2 + e * q)
    square = alpha * alpha
    beta = square * uu / m
    curve = square * ulu - beta * beta * q
    alpha_next = square * uu / curve
    c0 = alpha + alpha_next * (1.0 + beta)
    c1 = -alpha_next * alpha
    wide0 = jnp.broadcast_to(c0, (16, 128))
    wide1 = jnp.broadcast_to(c1, (16, 128))
    for i in range(8):
        p_ref[i] = wide0 * v0_ref[i] + wide1 * v1_ref[i]
    p_copy = pltpu.make_async_copy(p_ref, p_out, sems.at[0])
    p_copy.start()
    loads = c0 * total + c1 * pltpu.roll(total, 104, 1)
    state = motion_ref[0:1, :] + motion_ref[1:2, :] * loads
    stores = store_ref[...]
    maps = []
    for c in range(6):
        value = jnp.zeros((32, 128), F32)
        for store in range(4):
            at = 8 + 4 * c + store
            value = jnp.where(stores == store, state[:, at : at + 1], value)
        maps.append(value)
    arms = [arm_ref[c] for c in range(3)]
    for c in range(3):
        a, b = (c + 1) % 3, (c + 2) % 3
        velocity_ref[c] = maps[c] + (maps[3 + a] * arms[b] - maps[3 + b] * arms[a])
    velocity_copy = pltpu.make_async_copy(velocity_ref, velocity_out, sems.at[1])
    velocity_copy.start()
    p_copy.wait()
    velocity_copy.wait()


def spread_geometry(geo_ref, out_ref):
    element = lax.broadcasted_iota(jnp.int32, (16, 128), 0)
    out_ref[...] = dot(geo_ref[...], jnp.where((lane_ids(16) >> 3) == element, 1.0, 0.0))


def wall_table(
    elem_ref, face_ref, stores_ref, motion_ref, inverse_ref, weight_ref, arm_ref,
    table_ref, code_ref, store_out, motion_out,
):
    weight = weight_ref[...]
    nodes = jnp.concatenate([weight] + [weight * arm_ref[c] for c in range(3)], axis=0)
    a = lax.broadcasted_iota(jnp.int32, (128, 128), 0)
    b = lax.broadcasted_iota(jnp.int32, (128, 128), 1)
    slot, outer, inner = a & 64, (a >> 3) & 7, a & 7
    table_ref[0:128, :] = dot(nodes, jnp.where(b == slot + (7 - outer) * 8 + inner, 1.0, 0.0))
    table_ref[128:256, :] = dot(nodes, jnp.where(b == slot + (7 - inner) * 8 + outer, 1.0, 0.0))

    elem, face, stores = elem_ref[...], face_ref[...], stores_ref[...]
    n = lax.broadcasted_iota(jnp.int32, (1, 64), 1)
    direction = face >> 1
    first = jnp.where(direction == 2, 128, 0) + (n >> 1)
    column = elem & 15
    code_ref[0:1, :] = ((2 * face + (elem >> 4)) * 5 + stores) * 3
    code_ref[1:2, :] = column
    code_ref[2:3, :] = (8 * column + 64 * (n & 1) + 72) & 127
    code_ref[3:4, :] = first
    code_ref[4:5, :] = first + jnp.where(direction == 2, 64, 96)
    code_ref[5:6, :] = first + jnp.where(direction == 0, 64, 32)
    code_ref[6:8, :] = jnp.zeros((2, 64), jnp.int32)

    numbers = stores.astype(F32)
    row = lax.broadcasted_iota(jnp.int32, (32, 64), 0)
    column = lax.broadcasted_iota(jnp.int32, (32, 64), 1)
    even = jnp.sum(jnp.where(column == 2 * row, numbers, 0.0), axis=1, keepdims=True)
    odd = jnp.sum(jnp.where(column == 2 * row + 1, numbers, 0.0), axis=1, keepdims=True)
    store_out[...] = jnp.where(lane_ids(32) < 64, even, odd)

    load = lane_ids(8) - 8
    inside = (load >= 0) & (load < 24)
    component, store = load >> 2, load & 3
    row = row_ids()
    motion = dot(motion_ref[...], jnp.where(inside & (component == row), 1.0, 0.0)[0:6, :])
    motion_out[0:1, :] = jnp.sum(jnp.where((store == row)[0:4, :], motion, 0.0), axis=0, keepdims=True)
    scale = dot(inverse_ref[...], jnp.where(inside & (store == row), 1.0, 0.0)[0:4, :])
    taken = jnp.maximum(component - 2, 0) == row
    motion_out[1:2, :] = jnp.sum(jnp.where(taken[0:4, :], scale, 0.0), axis=0, keepdims=True)


def wall_weights(begin, end, code_ref, table_ref, *rest):
    omega_ref = rest[-1]
    if begin == 0:
        omega_ref[...] = jnp.zeros(omega_ref.shape, F32)
    lane = lane_ids() >> 3

    def add(step, carry):
        tiles = []
        for k in range(8):
            n = begin + 8 * step + k
            here = lane == code_ref[1, n]
            for q in range(3):
                nodes = jnp.broadcast_to(table_ref[pl.ds(code_ref[3 + q, n], 1), :], (8, 128))
                nodes = pltpu.roll(pltpu.roll(nodes, 0, 1, stride=8, stride_axis=0), code_ref[2, n], 1)
                tiles.append(jnp.where(here, nodes, 0.0))
        for k in range(8):
            at = code_ref[0, begin + 8 * step + k]
            for q in range(3):
                omega_ref[at + q] += tiles[3 * k + q]
        return carry

    lax.fori_loop(0, (end - begin) // 8, add, 0)


def shifted(x, axis, step, ring=False):
    count = lax.axis_size(axis)
    pairs = [(i, (i + step) % count) for i in range(count) if ring or 0 <= i + step < count]
    return lax.ppermute(x, axis, pairs)


def swapped(x, axis, first):
    pairs = [(i, i + 1) for i in range(first, lax.axis_size(axis) - 1, 2)]
    return lax.ppermute(x, axis, pairs + [(b, a) for a, b in pairs])


SWAPS = "ACD"
SPLIT = 32


STAGES = ((("vert", "span"), 32, 22), ("stream", 16, 8))


def reduced(sums):
    for at, (axes, count, first) in enumerate(STAGES):
        lists = [[(first + n) % count for n in range(count)]]
        sums = lax.all_to_all(sums.reshape(count, 1, 128), axes, 0, 0, axis_index_groups=lists).reshape(count, 128)
        if at == 0:
            sums = call(group_sums, [(STAGES[1][1], 128)])(sums)[0]
    return sums


AXIS = {"A": "stream", "B": "vert", "C": "span", "D": "stream"}
FLIPS = "D"


def swaps_at(stage):
    return int(stage in FLIPS)


def exchange(one, two, stage):
    axis = AXIS[stage]
    if stage in SWAPS:
        first = swaps_at(stage)
        return swapped(one, axis, first), swapped(two, axis, 1 - first)
    return shifted(one, axis, 1, stage == "B"), shifted(two, axis, -1, stage == "B")


def in_order(first, second, stage):
    if stage not in SWAPS:
        return first, second
    even = lax.axis_index(AXIS[stage]) % 2 == swaps_at(stage)
    return jnp.where(even, second, first), jnp.where(even, first, second)


def sent_in_order(up, down, stage):
    if stage not in SWAPS:
        return up, down
    even = lax.axis_index(AXIS[stage]) % 2 == swaps_at(stage)
    return jnp.where(even, up, down), jnp.where(even, down, up)


def per_device(
    forcing, geometry, wall_elem, wall_face, wall_store, wall_weight, wall_arm, store_motion, store_inverse
):
    lane_k, lane_i, rows, node_w = [jnp.asarray(a) for a in constants()]
    field = (8, 16, 128)
    tie = lax.optimization_barrier

    if "A" in SWAPS:
        odd = (lax.axis_index("stream") + swaps_at("A")) % 2
        top, bottom = [lax.dynamic_index_in_dim(forcing, at, 0, False) for at in (7 - 7 * odd, 7 * odd)]
    else:
        top, bottom = forcing[7], forcing[0]
    low, high = exchange(top, bottom, "A")
    geo = call(spread_geometry, [(8, 128)])(geometry.reshape(8, 16))[0]
    x, up, down = call(stream_added, [field, (72, 128), (72, 128)])(forcing, low, high, geo)

    up, down, weight, arms = tie((up, down, wall_weight.reshape(32, 128), wall_arm.reshape(3, 32, 128)))
    low, high = exchange(up, down, "B")
    table, codes, store_rows, motion = call(
        wall_table, [(256, 128), ((8, 64), jnp.int32), (32, 128), (2, 128)]
    )(wall_elem, wall_face, wall_store, store_motion.T, store_inverse, weight, arms)
    omega = call(functools.partial(wall_weights, 0, SPLIT), [(180, 8, 128)])(codes, table, smem=1)[0]
    low, high, table, codes, omega = tie((low, high, table, codes, omega))
    wide, geo_wide, right, left, to_one, to_two = call(vert_added, [(8, 32, 128), (16, 128)] + [(48, 128)] * 4)(
        x, low, high, geo
    )

    to_one, to_two, table, codes, omega = tie((to_one, to_two, table, codes, omega))
    low, high = exchange(to_one, to_two, "C")
    omega = call(functools.partial(wall_weights, SPLIT, 64), [(180, 8, 128)], input_output_aliases={2: 0})(
        codes, table, omega, smem=1
    )[0]
    low, high, omega = tie((low, high, omega))
    v0, local, part, top, bottom, maps = call(
        span_added,
        [field, field, field, (16, 128), (16, 128), (4, 16, 128)],
        scratch_shapes=[pltpu.VMEM((288, 128), F32)],
    )(wide, geo_wide, right, left, low, high, lane_k, lane_i, rows, node_w)

    low, high = exchange(top, bottom, "D")
    pre = call(before_image, [(8, 128)])(v0, local, part, omega)[0]
    v1, sums = call(image_sums, [field, (STAGES[0][1], 128)], scratch_shapes=[pltpu.VMEM((128, 128), F32)])(
        v0, local, part, low, high, maps, omega, pre, lane_k, rows
    )
    sums = reduced(sums)
    pressure, velocity = call(
        finish,
        [field, (3, 32, 128)],
        out_space=pltpu.HBM,
        scratch_shapes=[pltpu.VMEM(field, F32), pltpu.VMEM((3, 32, 128), F32), pltpu.SemaphoreType.DMA((2,))],
    )(sums, v0, v1, arms, store_rows, motion)
    return pressure, velocity.reshape(1, 3, 4096)


def solution(mesh):
    return jax.shard_map(
        per_device,
        mesh=mesh,
        in_specs=(
            P("stream", "vert", "span"),
            P(None, "stream", "vert", "span"),
            SHARDS,
            SHARDS,
            SHARDS,
            SHARDS,
            P(AXES, None, None),
            P(),
            P(),
        ),
        out_specs=(P("stream", "vert", "span"), P(AXES, None, None)),
        check_vma=False,
    )
```

```python
import functools

import jax
import jax.numpy as jnp
import numpy as np
from jax import lax
from jax.experimental import pallas as pl
from jax.experimental.pallas import tpu as pltpu
from jax.sharding import PartitionSpec as P

F32 = jnp.float32
UU, G2, M, ULU, T2, Q, S = range(7)
AXES = ("stream", "vert", "span")
SHARDS = P(AXES, None)
gll_inner = [
    -0.8717401485096066,
    -0.5917001814331423,
    -0.2092992179024789,
    0.2092992179024789,
    0.5917001814331423,
    0.8717401485096066,
]
MOMENTS = (((1, 2, 1.0), (2, 1, -1.0)), ((0, 2, -1.0), (2, 0, 1.0)), ((0, 1, 1.0), (1, 0, -1.0)))


def legendre_seven(points):
    before = points * 0.0 + 1.0
    current = points * 1.0
    for order in range(1, 7):
        following = ((2 * order + 1) * points * current - order * before) / (order + 1)
        before = current
        current = following
    return current


def gll_tables():
    degree = 7
    points = np.array([-1.0] + gll_inner + [1.0])
    legendre_at = legendre_seven(points)
    weights = 2.0 / (degree * (degree + 1) * legendre_at**2)
    derivative = np.zeros((8, 8))
    for i in range(8):
        for j in range(8):
            if i != j:
                derivative[i, j] = legendre_at[i] / (legendre_at[j] * (points[i] - points[j]))
    derivative[0, 0] = -degree * (degree + 1) / 4.0
    derivative[7, 7] = degree * (degree + 1) / 4.0
    return derivative, weights


DERIV, WEIGHTS = gll_tables()
STIFF = DERIV.T @ np.diag(WEIGHTS) @ DERIV


def constants():
    def f32(a):
        return np.asarray(a, np.float32)

    lane_k = f32(np.kron(np.eye(16), STIFF))
    lane_i = f32(np.kron(np.eye(2), np.kron(STIFF, np.eye(8))))
    rows = f32(np.kron(np.eye(32), STIFF))
    wj = np.tile(WEIGHTS[:, None], (1, 128))
    wk = np.tile(np.tile(WEIGHTS, 16)[None], (8, 1))
    wi = np.tile(np.tile(np.repeat(WEIGHTS, 8), 2)[None], (8, 1))
    return lane_k, lane_i, rows, f32(np.concatenate([wj, wk, wi], axis=0))


def dot(a, b):
    return lax.dot_general(
        a,
        b,
        (((1,), (0,)), ((), ())),
        precision=lax.Precision.HIGHEST,
        preferred_element_type=F32,
    )


def lane_sums(rows, first):
    n = rows.shape[0]
    sums = jnp.sum(rows, axis=1, keepdims=True)
    place = lax.broadcasted_iota(jnp.int32, (n, 128), 0) + first
    return jnp.sum(jnp.where(lane_ids(n) == place, sums, 0.0), axis=0, keepdims=True)


def row_ids():
    return lax.broadcasted_iota(jnp.int32, (8, 128), 0)


def lane_ids(rows=8):
    return lax.broadcasted_iota(jnp.int32, (rows, 128), 1)


def join_rows(below, above):
    row = row_ids()
    new_below = below + jnp.where(row == 7, pltpu.roll(above, 7, 0), 0.0)
    new_above = above + jnp.where(row == 0, pltpu.roll(below, 1, 0), 0.0)
    return new_below, new_above


def join_lanes(tile):
    lane = lane_ids()
    k = lane % 8
    left = jnp.where((k == 0) & (lane > 0), pltpu.roll(tile, 1, 1), 0.0)
    right = jnp.where((k == 7) & (lane < 127), pltpu.roll(tile, 127, 1), 0.0)
    return tile + left + right


def call(body, outs, cost=2000, space=pltpu.VMEM, out_space=pltpu.VMEM, **kwargs):
    given, taken = pl.BlockSpec(memory_space=space), pl.BlockSpec(memory_space=out_space)

    shapes = [s if isinstance(s[0], tuple) else (s, F32) for s in outs]

    def run(*args, smem=0):
        specs = [pl.BlockSpec(memory_space=pltpu.SMEM)] * smem + [given] * (len(args) - smem)
        return pl.pallas_call(
            body,
            out_shape=[jax.ShapeDtypeStruct(*s) for s in shapes],
            in_specs=specs,
            out_specs=[taken] * len(outs),
            compiler_params=pltpu.CompilerParams(vmem_limit_bytes=16 * 2**20),
            cost_estimate=pl.CostEstimate(flops=cost * 1000, bytes_accessed=200000, transcendentals=0),
            **kwargs,
        )(*args)

    return run


def stream_added(f_ref, low_ref, high_ref, geo_ref, x_ref, up_ref, down_ref):
    low, high = in_order(low_ref[...], high_ref[...], "A")
    for i in range(8):
        a = f_ref[i, 0:8, :]
        b = f_ref[i, 8:16, :]
        if i == 0:
            a = a + low[0:8, :]
            b = b + low[8:16, :]
        if i == 7:
            a = a + high[0:8, :]
            b = b + high[8:16, :]
        a, b = join_rows(a, b)
        x_ref[i, 0:8, :] = a
        x_ref[i, 8:16, :] = b
        one, two = sent_in_order(b, a, "B")
        up_ref[8 * i : 8 * i + 8, :] = one
        down_ref[8 * i : 8 * i + 8, :] = two
    down_ref[64:72, :] = geo_ref[...]
    up_ref[64:72, :] = geo_ref[...]


def vert_added(x_ref, low_ref, high_ref, geo_ref, v_ref, g_ref, right_ref, left_ref, one_ref, two_ref):
    v = lax.axis_index("vert")
    has_low = jnp.where(v > 0, 1.0, 0.0)
    has_high = jnp.where(v < 7, 1.0, 0.0)
    lane = lane_ids()
    right = [jnp.zeros((8, 128), F32) for _ in range(4)]
    left = [jnp.zeros((8, 128), F32) for _ in range(4)]
    for i in range(8):
        rows = slice(8 * i, 8 * i + 8)
        low, high = in_order(low_ref[rows, :], high_ref[rows, :], "B")
        low, a = join_rows(low * has_low, x_ref[i, 0:8, :])
        b, high = join_rows(x_ref[i, 8:16, :], high * has_high)
        for t, tile in enumerate((low, a, b, high)):
            tile = join_lanes(tile)
            v_ref[i, 8 * t : 8 * t + 8, :] = tile
            to_right = pltpu.roll(tile, (8 * i - 120) % 128, 1)
            to_left = pltpu.roll(tile, 64 + 8 * i, 1)
            right[t] = jnp.where(lane // 8 == i, to_right, right[t])
            left[t] = jnp.where(lane // 8 == 8 + i, to_left, left[t])
    for t in range(4):
        right_ref[8 * t : 8 * t + 8, :] = right[t]
        left_ref[8 * t : 8 * t + 8, :] = left[t]
    geo = geo_ref[...]
    geo_low, geo_high = in_order(low_ref[64:72, :], high_ref[64:72, :], "B")
    geo_low, geo_high = geo_low * has_low, geo_high * has_high
    rows = []
    for d in range(4):
        rows.append(geo_low[2 * d + 1 : 2 * d + 2, :])
        rows.append(geo[2 * d : 2 * d + 2, :])
        rows.append(geo_high[2 * d : 2 * d + 1, :])
    extended = jnp.concatenate(rows, axis=0)
    g_ref[...] = extended
    wide = lane_ids(16)
    last = jnp.broadcast_to(extended[:, 127:128], (16, 128))
    first = jnp.broadcast_to(extended[:, 0:1], (16, 128))
    right_ref[32:48, :] = jnp.where(wide < 64, last, 0.0)
    left_ref[32:48, :] = jnp.where(wide >= 64, first, 0.0)
    one_ref[...], two_ref[...] = sent_in_order(right_ref[...], left_ref[...], "C")


def node_rows(geo, d, t):
    return jnp.broadcast_to(geo[4 * d + t : 4 * d + t + 1, :], (8, 128))


def span_added(
    v_ref, g_ref, right_ref, left_ref, low_ref, high_ref, kk_ref, ki_ref, kr_ref, w_ref,
    v0_ref, local_ref, part_ref, top_ref, bottom_ref, maps_ref, field,
):
    lane = lane_ids()
    wj, wk, wi = w_ref[0:8, :], w_ref[8:16, :], w_ref[16:24, :]
    got = [low_ref[8 * t : 8 * t + 8, :] + high_ref[8 * t : 8 * t + 8, :] for t in range(4)]
    halo = []
    for t in range(4):
        rows = slice(8 * t, 8 * t + 8)
        from_own_first = pltpu.roll(left_ref[rows, :], 71, 1)
        from_own_last = pltpu.roll(right_ref[rows, :], 57, 1)
        tile = got[t] + jnp.where((lane < 64) & (lane % 8 == 7), from_own_first, 0.0)
        halo.append(tile + jnp.where((lane >= 64) & (lane % 8 == 0), from_own_last, 0.0))
    own = [[None] * 4 for _ in range(8)]
    for i in range(8):
        for t in range(4):
            first = pltpu.roll(got[t], (-(8 * i + 7)) % 128, 1)
            last = pltpu.roll(got[t], (63 - 8 * i) % 128, 1)
            tile = v_ref[i, 8 * t : 8 * t + 8, :]
            tile = tile + jnp.where(lane == 0, first, 0.0) + jnp.where(lane == 127, last, 0.0)
            own[i][t] = tile
            field[32 * i + 8 * t : 32 * i + 8 * t + 8, :] = tile
        v0_ref[i, 0:8, :] = own[i][1]
        v0_ref[i, 8:16, :] = own[i][2]
    for t in range(4):
        field[256 + 8 * t : 264 + 8 * t, :] = halo[t]
    along_k = dot(field[...], kk_ref[...])
    along_j = dot(kr_ref[...], field[0:256, :])
    halo_j = dot(kr_ref[0:32, 0:32], field[256:288, :])
    halo_i = dot(field[256:288, :], ki_ref[...])

    geo = g_ref[...]
    geo_halo = low_ref[32:48, :] + high_ref[32:48, :]
    out = [[None] * 4 for _ in range(8)]
    out_halo = []
    for t in range(4):
        g0, g1, g2, g3 = [node_rows(geo, d, t) for d in range(4)]
        f0, f1, f2, f3 = g0 * wj * wk, g1 * wk, g2 * wj, 50.0 * g3 * wj * wk
        if t in (1, 2):
            for d, f in enumerate((f0, f1, f2, f3)):
                maps_ref[d, 8 * t - 8 : 8 * t, :] = f
        for i in range(8):
            along_i = own[0][t] * float(STIFF[i, 0])
            for q in range(1, 8):
                along_i = along_i + own[q][t] * float(STIFF[i, q])
            at = slice(32 * i + 8 * t, 32 * i + 8 * t + 8)
            inner = f1 * along_j[at, :] + f2 * along_k[at, :] + f3 * own[i][t]
            out[i][t] = f0 * along_i + float(WEIGHTS[i]) * inner
        h0, h1, h2, h3 = [node_rows(geo_halo, d, t) for d in range(4)]
        at = slice(8 * t, 8 * t + 8)
        total = h0 * wj * wk * halo_i[at, :] + h1 * wi * wk * halo_j[at, :]
        total = total + h2 * wi * wj * along_k[256 + 8 * t : 264 + 8 * t, :]
        out_halo.append(total + 50.0 * h3 * wi * wj * wk * halo[t])

    row = row_ids()

    def middle(tiles):
        low, a, b, high = tiles
        new_a = a + jnp.where(row == 0, pltpu.roll(low, 1, 0), 0.0) + jnp.where(row == 7, pltpu.roll(b, 7, 0), 0.0)
        new_b = b + jnp.where(row == 0, pltpu.roll(a, 1, 0), 0.0) + jnp.where(row == 7, pltpu.roll(high, 7, 0), 0.0)
        return new_a, new_b

    beside = middle(out_halo)
    outer = {0: [], 7: []}
    for i in range(8):
        local_ref[i, 0:8, :] = out[i][1]
        local_ref[i, 8:16, :] = out[i][2]
        for b, tile in enumerate(middle(out[i])):
            tile = join_lanes(tile)
            first = pltpu.roll(beside[b], (-(8 * i + 7)) % 128, 1)
            last = pltpu.roll(beside[b], (63 - 8 * i) % 128, 1)
            tile = tile + jnp.where(lane == 0, first, 0.0) + jnp.where(lane == 127, last, 0.0)
            part_ref[i, 8 * b : 8 * b + 8, :] = tile
            if i in (0, 7):
                outer[i].append(tile)
    top, bottom = [jnp.concatenate(outer[i], axis=0) for i in (7, 0)]
    top_ref[...], bottom_ref[...] = sent_in_order(top, bottom, "D")


def share_maps():
    s, v, w = [lax.axis_index(a) for a in AXES]
    row, lane = row_ids(), lane_ids()
    k = lane % 8
    shared = ((k == 0) & ((lane > 0) | (w > 0))) | ((k == 7) & ((lane < 127) | (w < 3)))
    span = jnp.where(shared, 0.5, 1.0)
    first = ((row == 0) & (v > 0)) | (row == 7)
    second = (row == 0) | ((row == 7) & (v < 7))
    tiles = (jnp.where(first, 0.5, 1.0) * span, jnp.where(second, 0.5, 1.0) * span)
    low = jnp.where(s > 0, 0.5, 1.0)
    high = jnp.where(s < 15, 0.5, 1.0)
    return tiles, [low] + [1.0] * 6 + [high]


def face_tiles(tiles):
    lane, row = lane_ids(), row_ids()
    out = []
    for side in range(2):
        out += [tiles[7 * side][0], tiles[7 * side][1]]
    for side in range(2):
        for b in range(2):
            tile = jnp.zeros((8, 128), F32)
            for i in range(8):
                tile = jnp.where(row == i, pltpu.roll(tiles[i][b], (i - 7 * side) % 8, 0), tile)
            out.append(tile)
    for side in range(2):
        for b in range(2):
            tile = jnp.zeros((8, 128), F32)
            for i in range(8):
                tile = jnp.where(lane % 8 == i, pltpu.roll(tiles[i][b], (i - 7 * side) % 128, 1), tile)
            out.append(tile)
    return [tile if (n // 2) % 2 == 0 else -tile for n, tile in enumerate(out)]


def load_rows(faces, omega_ref):
    sums = [[None] * 4 for _ in range(6)]
    for d in range(3):
        targets = [(d, 1.0)] + [(3 + c, sign) for c, _, sign in MOMENTS[d]]
        for q, (component, sign) in enumerate(targets):
            for store in range(4):
                total = None
                for face in (2 * d, 2 * d + 1):
                    for b in range(2):
                        term = omega_ref[((2 * face + b) * 5 + store) * 3 + q] * faces[2 * face + b]
                        total = term if total is None else total + term
                total = total * sign
                before = sums[component][store]
                sums[component][store] = total if before is None else before + total
    return [jnp.sum(sums[c][s], axis=0, keepdims=True) for c in range(6) for s in range(4)]


def zero_rows(n):
    return [jnp.zeros((n, 128), F32)]


def sublane_sum(tile):
    return jnp.sum(tile, axis=0, keepdims=True)


def before_image(v0_ref, local_ref, part_ref, omega_ref, pre_ref):
    share, layers = share_maps()
    norm = energy = top = bottom = jnp.zeros((8, 128), F32)
    tiles = [[v0_ref[i, 0:8, :], v0_ref[i, 8:16, :]] for i in range(8)]
    for i in range(8):
        for b in range(2):
            x = tiles[i][b]
            square = x * x * share[b]
            norm = norm + square * layers[i]
            energy = energy + x * local_ref[i, 8 * b : 8 * b + 8, :]
            if 0 < i < 7:
                bottom = bottom + square
                top = top + x * part_ref[i, 8 * b : 8 * b + 8, :] * share[b]
    rows = [sublane_sum(top), sublane_sum(norm), sublane_sum(bottom)] + zero_rows(1)
    rows += [sublane_sum(energy)] + zero_rows(3) + load_rows(face_tiles(tiles), omega_ref)
    sums = lane_sums(jnp.concatenate(rows, axis=0), 0)
    lane = lane_ids(1)
    over, norm, under, energy = sums[:, 0:1], sums[:, 1:2], sums[:, 2:3], sums[:, 4:5]
    usable = under > 1e-30
    quotient = jnp.where(usable, over / jnp.where(usable, under, 1.0), 0.0)
    quotient = jnp.clip(quotient, 0.0, 1e6)
    row = jnp.where(lane >= 8, sums, 0.0)
    for n, value in ((M, norm), (Q, energy), (S, quotient)):
        row = jnp.where(lane == n, value, row)
    pre_ref[...] = jnp.broadcast_to(row, (8, 128))


def image_sums(
    v0_ref, local_ref, part_ref, low_ref, high_ref, maps_ref, omega_ref, pre_ref, kk_ref, kr_ref,
    v1_ref, out_ref, field,
):
    share, layers = share_maps()
    low, high = in_order(low_ref[...], high_ref[...], "D")
    quotient = jnp.broadcast_to(pre_ref[:, S : S + 1], (8, 128))
    v1 = [[None] * 2 for _ in range(8)]
    u = [[None] * 2 for _ in range(8)]
    norm = cross_norm = energy = cross_energy = jnp.zeros((8, 128), F32)
    for i in range(8):
        for b in range(2):
            rows = slice(8 * b, 8 * b + 8)
            tile = part_ref[i, rows, :]
            if i == 0:
                tile = tile + low[rows, :]
            if i == 7:
                tile = tile + high[rows, :]
            v1[i][b] = tile
            v1_ref[i, rows, :] = tile
            x = v0_ref[i, rows, :]
            y = tile - quotient * x
            u[i][b] = y
            field[16 * i + 8 * b : 16 * i + 8 * b + 8, :] = y
            weighted = y * share[b] * layers[i]
            norm = norm + y * weighted
            cross_norm = cross_norm + x * weighted
            cross_energy = cross_energy + y * local_ref[i, rows, :]
    along_k = dot(field[...], kk_ref[...])
    along_j = dot(kr_ref[0:128, 0:128], field[...])
    for b in range(2):
        rows = slice(8 * b, 8 * b + 8)
        f0, f1, f2, f3 = [maps_ref[d, rows, :] for d in range(4)]
        for i in range(8):
            along_i = u[0][b] * float(STIFF[i, 0])
            for q in range(1, 8):
                along_i = along_i + u[q][b] * float(STIFF[i, q])
            at = slice(16 * i + 8 * b, 16 * i + 8 * b + 8)
            inner = f1 * along_j[at, :] + f2 * along_k[at, :] + f3 * u[i][b]
            energy = energy + u[i][b] * (f0 * along_i + float(WEIGHTS[i]) * inner)
    rows = [sublane_sum(a) for a in (norm, 2.0 * cross_norm)] + zero_rows(1)
    rows += [sublane_sum(a) for a in (energy, 2.0 * cross_energy)] + zero_rows(3)
    row = lane_sums(jnp.concatenate(rows, axis=0), 0)
    row = row + lane_sums(jnp.concatenate(load_rows(face_tiles(v1), omega_ref), axis=0), 32)
    out_ref[...] = jnp.broadcast_to(row + pre_ref[0:1, :], out_ref.shape)


def merged(parts):
    n = parts.shape[0]
    lane = lane_ids(n)
    common = parts[0:1, S : S + 1]
    e = parts[:, S : S + 1] - common
    once = jnp.where((lane == UU) | (lane == ULU), 1.0, jnp.where((lane == G2) | (lane == T2), 2.0, 0.0))
    twice = jnp.where((lane == UU) | (lane == ULU), 1.0, 0.0)
    rows = parts + e * (once * pltpu.roll(parts, 127, 1) + e * (twice * pltpu.roll(parts, 126, 1)))
    total = jnp.sum(rows, axis=0, keepdims=True)
    return jnp.where(lane_ids(1) == S, common, total)


def group_sums(parts_ref, out_ref):
    out_ref[...] = jnp.broadcast_to(merged(parts_ref[...]), out_ref.shape)


def load_column(row, first):
    place = lax.broadcasted_iota(jnp.int32, (24, 128), 0) + first
    return jnp.sum(jnp.where(lane_ids(24) == place, row, 0.0), axis=1, keepdims=True)


def finish(
    parts_ref, v0_ref, v1_ref, arm_ref, store_ref, motion_ref, p_out, velocity_out, p_ref, velocity_ref, sems
):
    total = merged(parts_ref[...])
    uu, g2, m, ulu, t2, q, s = [total[:, n : n + 1] for n in range(7)]
    alpha = m / q
    e = s - q / m
    uu = uu + e * (g2 + e * m)
    ulu = ulu + e * (t2 + e * q)
    square = alpha * alpha
    beta = square * uu / m
    curve = square * ulu - beta * beta * q
    alpha_next = square * uu / curve
    c0 = alpha + alpha_next * (1.0 + beta)
    c1 = -alpha_next * alpha
    wide0 = jnp.broadcast_to(c0, (16, 128))
    wide1 = jnp.broadcast_to(c1, (16, 128))
    for i in range(8):
        p_ref[i] = wide0 * v0_ref[i] + wide1 * v1_ref[i]
    p_copy = pltpu.make_async_copy(p_ref, p_out, sems.at[0])
    p_copy.start()
    loads = c0 * load_column(total, 8) + c1 * load_column(total, 32)
    state = motion_ref[0:24, :] + motion_ref[24:48, :] * loads
    stores = store_ref[...]
    maps = []
    for c in range(6):
        value = jnp.zeros((32, 128), F32)
        for store in range(4):
            at = 4 * c + store
            value = jnp.where(stores == store, state[at : at + 1, :], value)
        maps.append(value)
    arms = [arm_ref[c] for c in range(3)]
    for c in range(3):
        a, b = (c + 1) % 3, (c + 2) % 3
        velocity_ref[c] = maps[c] + (maps[3 + a] * arms[b] - maps[3 + b] * arms[a])
    velocity_copy = pltpu.make_async_copy(velocity_ref, velocity_out, sems.at[1])
    velocity_copy.start()
    p_copy.wait()
    velocity_copy.wait()


def spread_geometry(geo_ref, out_ref):
    element = lax.broadcasted_iota(jnp.int32, (16, 128), 0)
    out_ref[...] = dot(geo_ref[...], jnp.where((lane_ids(16) >> 3) == element, 1.0, 0.0))


def wall_table(
    elem_ref, face_ref, stores_ref, motion_ref, inverse_ref, weight_ref, arm_ref,
    table_ref, code_ref, store_out, motion_out,
):
    weight = weight_ref[...]
    nodes = jnp.concatenate([weight] + [weight * arm_ref[c] for c in range(3)], axis=0)
    a = lax.broadcasted_iota(jnp.int32, (128, 128), 0)
    b = lax.broadcasted_iota(jnp.int32, (128, 128), 1)
    slot, outer, inner = a & 64, (a >> 3) & 7, a & 7
    table_ref[0:128, :] = dot(nodes, jnp.where(b == slot + (7 - outer) * 8 + inner, 1.0, 0.0))
    table_ref[128:256, :] = dot(nodes, jnp.where(b == slot + (7 - inner) * 8 + outer, 1.0, 0.0))

    elem, face, stores = elem_ref[...], face_ref[...], stores_ref[...]
    n = lax.broadcasted_iota(jnp.int32, (1, 64), 1)
    direction = face >> 1
    first = jnp.where(direction == 2, 128, 0) + (n >> 1)
    column = elem & 15
    code_ref[0:1, :] = ((2 * face + (elem >> 4)) * 5 + stores) * 3
    code_ref[1:2, :] = column
    code_ref[2:3, :] = (8 * column + 64 * (n & 1) + 72) & 127
    code_ref[3:4, :] = first
    code_ref[4:5, :] = first + jnp.where(direction == 2, 64, 96)
    code_ref[5:6, :] = first + jnp.where(direction == 0, 64, 32)
    code_ref[6:8, :] = jnp.zeros((2, 64), jnp.int32)

    numbers = stores.astype(F32)
    row = lax.broadcasted_iota(jnp.int32, (32, 64), 0)
    column = lax.broadcasted_iota(jnp.int32, (32, 64), 1)
    even = jnp.sum(jnp.where(column == 2 * row, numbers, 0.0), axis=1, keepdims=True)
    odd = jnp.sum(jnp.where(column == 2 * row + 1, numbers, 0.0), axis=1, keepdims=True)
    store_out[...] = jnp.where(lane_ids(32) < 64, even, odd)

    load = lane_ids(8) - 8
    inside = (load >= 0) & (load < 24)
    component, store = load >> 2, load & 3
    row = row_ids()
    motion = dot(motion_ref[...], jnp.where(inside & (component == row), 1.0, 0.0)[0:6, :])
    motion = jnp.sum(jnp.where((store == row)[0:4, :], motion, 0.0), axis=0, keepdims=True)
    motion_out[0:24, :] = jnp.broadcast_to(load_column(motion, 8), (24, 128))
    scale = dot(inverse_ref[...], jnp.where(inside & (store == row), 1.0, 0.0)[0:4, :])
    taken = jnp.maximum(component - 2, 0) == row
    scale = jnp.sum(jnp.where(taken[0:4, :], scale, 0.0), axis=0, keepdims=True)
    motion_out[24:48, :] = jnp.broadcast_to(load_column(scale, 8), (24, 128))


def wall_weights(begin, end, code_ref, table_ref, *rest):
    omega_ref = rest[-1]
    if begin == 0:
        omega_ref[...] = jnp.zeros(omega_ref.shape, F32)
    lane = lane_ids() >> 3

    def add(step, carry):
        tiles = []
        for k in range(8):
            n = begin + 8 * step + k
            here = lane == code_ref[1, n]
            for q in range(3):
                nodes = jnp.broadcast_to(table_ref[pl.ds(code_ref[3 + q, n], 1), :], (8, 128))
                nodes = pltpu.roll(pltpu.roll(nodes, 0, 1, stride=8, stride_axis=0), code_ref[2, n], 1)
                tiles.append(jnp.where(here, nodes, 0.0))
        for k in range(8):
            at = code_ref[0, begin + 8 * step + k]
            for q in range(3):
                omega_ref[at + q] += tiles[3 * k + q]
        return carry

    lax.fori_loop(0, (end - begin) // 8, add, 0)


def shifted(x, axis, step, ring=False):
    count = lax.axis_size(axis)
    pairs = [(i, (i + step) % count) for i in range(count) if ring or 0 <= i + step < count]
    return lax.ppermute(x, axis, pairs)


def swapped(x, axis, first):
    pairs = [(i, i + 1) for i in range(first, lax.axis_size(axis) - 1, 2)]
    return lax.ppermute(x, axis, pairs + [(b, a) for a, b in pairs])


SWAPS = "ACD"
SPLIT = 16


STAGES = ((("vert", "span"), 32, 22), ("stream", 16, 8))


def reduced(sums):
    for at, (axes, count, first) in enumerate(STAGES):
        lists = [[(first + n) % count for n in range(count)]]
        sums = lax.all_to_all(sums.reshape(count, 1, 128), axes, 0, 0, axis_index_groups=lists).reshape(count, 128)
        if at == 0:
            sums = call(group_sums, [(STAGES[1][1], 128)])(sums)[0]
    return sums


AXIS = {"A": "stream", "B": "vert", "C": "span", "D": "stream"}
FLIPS = "D"


def swaps_at(stage):
    return int(stage in FLIPS)


def exchange(one, two, stage):
    axis = AXIS[stage]
    if stage in SWAPS:
        first = swaps_at(stage)
        return swapped(one, axis, first), swapped(two, axis, 1 - first)
    return shifted(one, axis, 1, stage == "B"), shifted(two, axis, -1, stage == "B")


def in_order(first, second, stage):
    if stage not in SWAPS:
        return first, second
    even = lax.axis_index(AXIS[stage]) % 2 == swaps_at(stage)
    return jnp.where(even, second, first), jnp.where(even, first, second)


def sent_in_order(up, down, stage):
    if stage not in SWAPS:
        return up, down
    even = lax.axis_index(AXIS[stage]) % 2 == swaps_at(stage)
    return jnp.where(even, up, down), jnp.where(even, down, up)


def per_device(
    forcing, geometry, wall_elem, wall_face, wall_store, wall_weight, wall_arm, store_motion, store_inverse
):
    lane_k, lane_i, rows, node_w = [jnp.asarray(a) for a in constants()]
    field = (8, 16, 128)
    tie = lax.optimization_barrier

    if "A" in SWAPS:
        odd = (lax.axis_index("stream") + swaps_at("A")) % 2
        top, bottom = [lax.dynamic_index_in_dim(forcing, at, 0, False) for at in (7 - 7 * odd, 7 * odd)]
    else:
        top, bottom = forcing[7], forcing[0]
    low, high = exchange(top, bottom, "A")
    geo = call(spread_geometry, [(8, 128)])(geometry.reshape(8, 16))[0]
    x, up, down = call(stream_added, [field, (72, 128), (72, 128)])(forcing, low, high, geo)

    up, down, weight, arms = tie((up, down, wall_weight.reshape(32, 128), wall_arm.reshape(3, 32, 128)))
    low, high = exchange(up, down, "B")
    table, codes, store_rows, motion = call(
        wall_table, [(256, 128), ((8, 64), jnp.int32), (32, 128), (48, 128)]
    )(wall_elem, wall_face, wall_store, store_motion.T, store_inverse, weight, arms)
    omega = call(functools.partial(wall_weights, 0, SPLIT), [(180, 8, 128)])(codes, table, smem=1)[0]
    low, high, table, codes, omega = tie((low, high, table, codes, omega))
    wide, geo_wide, right, left, to_one, to_two = call(vert_added, [(8, 32, 128), (16, 128)] + [(48, 128)] * 4)(
        x, low, high, geo
    )

    to_one, to_two, table, codes, omega = tie((to_one, to_two, table, codes, omega))
    low, high = exchange(to_one, to_two, "C")
    omega = call(functools.partial(wall_weights, SPLIT, 64), [(180, 8, 128)], input_output_aliases={2: 0})(
        codes, table, omega, smem=1
    )[0]
    low, high, omega = tie((low, high, omega))
    v0, local, part, top, bottom, maps = call(
        span_added,
        [field, field, field, (16, 128), (16, 128), (4, 16, 128)],
        scratch_shapes=[pltpu.VMEM((288, 128), F32)],
    )(wide, geo_wide, right, left, low, high, lane_k, lane_i, rows, node_w)

    low, high = exchange(top, bottom, "D")
    pre = call(before_image, [(8, 128)])(v0, local, part, omega)[0]
    v1, sums = call(image_sums, [field, (STAGES[0][1], 128)], scratch_shapes=[pltpu.VMEM((128, 128), F32)])(
        v0, local, part, low, high, maps, omega, pre, lane_k, rows
    )
    sums = reduced(sums)
    pressure, velocity = call(
        finish,
        [field, (3, 32, 128)],
        out_space=pltpu.HBM,
        scratch_shapes=[pltpu.VMEM(field, F32), pltpu.VMEM((3, 32, 128), F32), pltpu.SemaphoreType.DMA((2,))],
    )(sums, v0, v1, arms, store_rows, motion)
    return pressure, velocity.reshape(1, 3, 4096)


def solution(mesh):
    return jax.shard_map(
        per_device,
        mesh=mesh,
        in_specs=(
            P("stream", "vert", "span"),
            P(None, "stream", "vert", "span"),
            SHARDS,
            SHARDS,
            SHARDS,
            SHARDS,
            P(AXES, None, None),
            P(),
            P(),
        ),
        out_specs=(P("stream", "vert", "span"), P(AXES, None, None)),
        check_vma=False,
    )
```

```python
import functools

import jax
import jax.numpy as jnp
import numpy as np
from jax import lax
from jax.experimental import pallas as pl
from jax.experimental.pallas import tpu as pltpu
from jax.sharding import PartitionSpec as P

F32 = jnp.float32
UU, G2, M, ULU, T2, Q, S = range(7)
AXES = ("stream", "vert", "span")
SHARDS = P(AXES, None)
gll_inner = [
    -0.8717401485096066,
    -0.5917001814331423,
    -0.2092992179024789,
    0.2092992179024789,
    0.5917001814331423,
    0.8717401485096066,
]
MOMENTS = (((1, 2, 1.0), (2, 1, -1.0)), ((0, 2, -1.0), (2, 0, 1.0)), ((0, 1, 1.0), (1, 0, -1.0)))


def legendre_seven(points):
    before = points * 0.0 + 1.0
    current = points * 1.0
    for order in range(1, 7):
        following = ((2 * order + 1) * points * current - order * before) / (order + 1)
        before = current
        current = following
    return current


def gll_tables():
    degree = 7
    points = np.array([-1.0] + gll_inner + [1.0])
    legendre_at = legendre_seven(points)
    weights = 2.0 / (degree * (degree + 1) * legendre_at**2)
    derivative = np.zeros((8, 8))
    for i in range(8):
        for j in range(8):
            if i != j:
                derivative[i, j] = legendre_at[i] / (legendre_at[j] * (points[i] - points[j]))
    derivative[0, 0] = -degree * (degree + 1) / 4.0
    derivative[7, 7] = degree * (degree + 1) / 4.0
    return derivative, weights


DERIV, WEIGHTS = gll_tables()
STIFF = DERIV.T @ np.diag(WEIGHTS) @ DERIV


def constants():
    def f32(a):
        return np.asarray(a, np.float32)

    lane_k = f32(np.kron(np.eye(16), STIFF))
    lane_i = f32(np.kron(np.eye(2), np.kron(STIFF, np.eye(8))))
    rows = f32(np.kron(np.eye(32), STIFF))
    wj = np.tile(WEIGHTS[:, None], (1, 128))
    wk = np.tile(np.tile(WEIGHTS, 16)[None], (8, 1))
    wi = np.tile(np.tile(np.repeat(WEIGHTS, 8), 2)[None], (8, 1))
    return lane_k, lane_i, rows, f32(np.concatenate([wj, wk, wi], axis=0))


def dot(a, b):
    return lax.dot_general(
        a,
        b,
        (((1,), (0,)), ((), ())),
        precision=lax.Precision.HIGHEST,
        preferred_element_type=F32,
    )


def lane_sums(rows, first):
    n = rows.shape[0]
    sums = jnp.sum(rows, axis=1, keepdims=True)
    place = lax.broadcasted_iota(jnp.int32, (n, 128), 0) + first
    return jnp.sum(jnp.where(lane_ids(n) == place, sums, 0.0), axis=0, keepdims=True)


def row_ids():
    return lax.broadcasted_iota(jnp.int32, (8, 128), 0)


def lane_ids(rows=8):
    return lax.broadcasted_iota(jnp.int32, (rows, 128), 1)


def join_rows(below, above):
    row = row_ids()
    new_below = below + jnp.where(row == 7, pltpu.roll(above, 7, 0), 0.0)
    new_above = above + jnp.where(row == 0, pltpu.roll(below, 1, 0), 0.0)
    return new_below, new_above


def join_lanes(tile):
    lane = lane_ids()
    k = lane % 8
    left = jnp.where((k == 0) & (lane > 0), pltpu.roll(tile, 1, 1), 0.0)
    right = jnp.where((k == 7) & (lane < 127), pltpu.roll(tile, 127, 1), 0.0)
    return tile + left + right


def call(body, outs, cost=2000, space=pltpu.VMEM, out_space=pltpu.VMEM, **kwargs):
    given, taken = pl.BlockSpec(memory_space=space), pl.BlockSpec(memory_space=out_space)

    shapes = [s if isinstance(s[0], tuple) else (s, F32) for s in outs]

    def run(*args, smem=0):
        specs = [pl.BlockSpec(memory_space=pltpu.SMEM)] * smem + [given] * (len(args) - smem)
        return pl.pallas_call(
            body,
            out_shape=[jax.ShapeDtypeStruct(*s) for s in shapes],
            in_specs=specs,
            out_specs=[taken] * len(outs),
            compiler_params=pltpu.CompilerParams(vmem_limit_bytes=16 * 2**20),
            cost_estimate=pl.CostEstimate(flops=cost * 1000, bytes_accessed=200000, transcendentals=0),
            **kwargs,
        )(*args)

    return run


def stream_added(f_ref, low_ref, high_ref, geo_ref, x_ref, up_ref, down_ref):
    low, high = in_order(low_ref[...], high_ref[...], "A")
    for i in range(8):
        a = f_ref[i, 0:8, :]
        b = f_ref[i, 8:16, :]
        if i == 0:
            a = a + low[0:8, :]
            b = b + low[8:16, :]
        if i == 7:
            a = a + high[0:8, :]
            b = b + high[8:16, :]
        a, b = join_rows(a, b)
        x_ref[i, 0:8, :] = a
        x_ref[i, 8:16, :] = b
        one, two = sent_in_order(b, a, "B")
        up_ref[8 * i : 8 * i + 8, :] = one
        down_ref[8 * i : 8 * i + 8, :] = two
    down_ref[64:72, :] = geo_ref[...]
    up_ref[64:72, :] = geo_ref[...]


def vert_added(x_ref, low_ref, high_ref, geo_ref, v_ref, g_ref, right_ref, left_ref, one_ref, two_ref):
    v = lax.axis_index("vert")
    has_low = jnp.where(v > 0, 1.0, 0.0)
    has_high = jnp.where(v < 7, 1.0, 0.0)
    lane = lane_ids()
    right = [jnp.zeros((8, 128), F32) for _ in range(4)]
    left = [jnp.zeros((8, 128), F32) for _ in range(4)]
    for i in range(8):
        rows = slice(8 * i, 8 * i + 8)
        low, high = in_order(low_ref[rows, :], high_ref[rows, :], "B")
        low, a = join_rows(low * has_low, x_ref[i, 0:8, :])
        b, high = join_rows(x_ref[i, 8:16, :], high * has_high)
        for t, tile in enumerate((low, a, b, high)):
            tile = join_lanes(tile)
            v_ref[i, 8 * t : 8 * t + 8, :] = tile
            to_right = pltpu.roll(tile, (8 * i - 120) % 128, 1)
            to_left = pltpu.roll(tile, 64 + 8 * i, 1)
            right[t] = jnp.where(lane // 8 == i, to_right, right[t])
            left[t] = jnp.where(lane // 8 == 8 + i, to_left, left[t])
    for t in range(4):
        right_ref[8 * t : 8 * t + 8, :] = right[t]
        left_ref[8 * t : 8 * t + 8, :] = left[t]
    geo = geo_ref[...]
    geo_low, geo_high = in_order(low_ref[64:72, :], high_ref[64:72, :], "B")
    geo_low, geo_high = geo_low * has_low, geo_high * has_high
    rows = []
    for d in range(4):
        rows.append(geo_low[2 * d + 1 : 2 * d + 2, :])
        rows.append(geo[2 * d : 2 * d + 2, :])
        rows.append(geo_high[2 * d : 2 * d + 1, :])
    extended = jnp.concatenate(rows, axis=0)
    g_ref[...] = extended
    wide = lane_ids(16)
    last = jnp.broadcast_to(extended[:, 127:128], (16, 128))
    first = jnp.broadcast_to(extended[:, 0:1], (16, 128))
    right_ref[32:48, :] = jnp.where(wide < 64, last, 0.0)
    left_ref[32:48, :] = jnp.where(wide >= 64, first, 0.0)
    one_ref[...], two_ref[...] = sent_in_order(right_ref[...], left_ref[...], "C")


def node_rows(geo, d, t):
    return jnp.broadcast_to(geo[4 * d + t : 4 * d + t + 1, :], (8, 128))


def span_added(
    v_ref, g_ref, right_ref, left_ref, low_ref, high_ref, kk_ref, ki_ref, kr_ref, w_ref,
    v0_ref, local_ref, part_ref, top_ref, bottom_ref, maps_ref, field,
):
    lane = lane_ids()
    wj, wk, wi = w_ref[0:8, :], w_ref[8:16, :], w_ref[16:24, :]
    got = [low_ref[8 * t : 8 * t + 8, :] + high_ref[8 * t : 8 * t + 8, :] for t in range(4)]
    halo = []
    for t in range(4):
        rows = slice(8 * t, 8 * t + 8)
        from_own_first = pltpu.roll(left_ref[rows, :], 71, 1)
        from_own_last = pltpu.roll(right_ref[rows, :], 57, 1)
        tile = got[t] + jnp.where((lane < 64) & (lane % 8 == 7), from_own_first, 0.0)
        halo.append(tile + jnp.where((lane >= 64) & (lane % 8 == 0), from_own_last, 0.0))
    own = [[None] * 4 for _ in range(8)]
    for i in range(8):
        for t in range(4):
            first = pltpu.roll(got[t], (-(8 * i + 7)) % 128, 1)
            last = pltpu.roll(got[t], (63 - 8 * i) % 128, 1)
            tile = v_ref[i, 8 * t : 8 * t + 8, :]
            tile = tile + jnp.where(lane == 0, first, 0.0) + jnp.where(lane == 127, last, 0.0)
            own[i][t] = tile
            field[32 * i + 8 * t : 32 * i + 8 * t + 8, :] = tile
        v0_ref[i, 0:8, :] = own[i][1]
        v0_ref[i, 8:16, :] = own[i][2]
    for t in range(4):
        field[256 + 8 * t : 264 + 8 * t, :] = halo[t]
    along_k = dot(field[...], kk_ref[...])
    along_j = dot(kr_ref[...], field[0:256, :])
    halo_j = dot(kr_ref[0:32, 0:32], field[256:288, :])
    halo_i = dot(field[256:288, :], ki_ref[...])

    geo = g_ref[...]
    geo_halo = low_ref[32:48, :] + high_ref[32:48, :]
    out = [[None] * 4 for _ in range(8)]
    out_halo = []
    for t in range(4):
        g0, g1, g2, g3 = [node_rows(geo, d, t) for d in range(4)]
        f0, f1, f2, f3 = g0 * wj * wk, g1 * wk, g2 * wj, 50.0 * g3 * wj * wk
        if t in (1, 2):
            for d, f in enumerate((f0, f1, f2, f3)):
                maps_ref[d, 8 * t - 8 : 8 * t, :] = f
        for i in range(8):
            along_i = own[0][t] * float(STIFF[i, 0])
            for q in range(1, 8):
                along_i = along_i + own[q][t] * float(STIFF[i, q])
            at = slice(32 * i + 8 * t, 32 * i + 8 * t + 8)
            inner = f1 * along_j[at, :] + f2 * along_k[at, :] + f3 * own[i][t]
            out[i][t] = f0 * along_i + float(WEIGHTS[i]) * inner
        h0, h1, h2, h3 = [node_rows(geo_halo, d, t) for d in range(4)]
        at = slice(8 * t, 8 * t + 8)
        total = h0 * wj * wk * halo_i[at, :] + h1 * wi * wk * halo_j[at, :]
        total = total + h2 * wi * wj * along_k[256 + 8 * t : 264 + 8 * t, :]
        out_halo.append(total + 50.0 * h3 * wi * wj * wk * halo[t])

    row = row_ids()

    def middle(tiles):
        low, a, b, high = tiles
        new_a = a + jnp.where(row == 0, pltpu.roll(low, 1, 0), 0.0) + jnp.where(row == 7, pltpu.roll(b, 7, 0), 0.0)
        new_b = b + jnp.where(row == 0, pltpu.roll(a, 1, 0), 0.0) + jnp.where(row == 7, pltpu.roll(high, 7, 0), 0.0)
        return new_a, new_b

    beside = middle(out_halo)
    outer = {0: [], 7: []}
    for i in range(8):
        local_ref[i, 0:8, :] = out[i][1]
        local_ref[i, 8:16, :] = out[i][2]
        for b, tile in enumerate(middle(out[i])):
            tile = join_lanes(tile)
            first = pltpu.roll(beside[b], (-(8 * i + 7)) % 128, 1)
            last = pltpu.roll(beside[b], (63 - 8 * i) % 128, 1)
            tile = tile + jnp.where(lane == 0, first, 0.0) + jnp.where(lane == 127, last, 0.0)
            part_ref[i, 8 * b : 8 * b + 8, :] = tile
            if i in (0, 7):
                outer[i].append(tile)
    top, bottom = [jnp.concatenate(outer[i], axis=0) for i in (7, 0)]
    top_ref[...], bottom_ref[...] = sent_in_order(top, bottom, "D")


def share_maps():
    s, v, w = [lax.axis_index(a) for a in AXES]
    row, lane = row_ids(), lane_ids()
    k = lane % 8
    shared = ((k == 0) & ((lane > 0) | (w > 0))) | ((k == 7) & ((lane < 127) | (w < 3)))
    span = jnp.where(shared, 0.5, 1.0)
    first = ((row == 0) & (v > 0)) | (row == 7)
    second = (row == 0) | ((row == 7) & (v < 7))
    tiles = (jnp.where(first, 0.5, 1.0) * span, jnp.where(second, 0.5, 1.0) * span)
    low = jnp.where(s > 0, 0.5, 1.0)
    high = jnp.where(s < 15, 0.5, 1.0)
    return tiles, [low] + [1.0] * 6 + [high]


def face_tiles(tiles):
    lane, row = lane_ids(), row_ids()
    out = []
    for side in range(2):
        out += [tiles[7 * side][0], tiles[7 * side][1]]
    for side in range(2):
        for b in range(2):
            tile = jnp.zeros((8, 128), F32)
            for i in range(8):
                tile = jnp.where(row == i, pltpu.roll(tiles[i][b], (i - 7 * side) % 8, 0), tile)
            out.append(tile)
    for side in range(2):
        for b in range(2):
            tile = jnp.zeros((8, 128), F32)
            for i in range(8):
                tile = jnp.where(lane % 8 == i, pltpu.roll(tiles[i][b], (i - 7 * side) % 128, 1), tile)
            out.append(tile)
    return [tile if (n // 2) % 2 == 0 else -tile for n, tile in enumerate(out)]


def load_rows(faces, omega_ref):
    sums = [[None] * 4 for _ in range(6)]
    for d in range(3):
        targets = [(d, 1.0)] + [(3 + c, sign) for c, _, sign in MOMENTS[d]]
        for q, (component, sign) in enumerate(targets):
            for store in range(4):
                total = None
                for face in (2 * d, 2 * d + 1):
                    for b in range(2):
                        term = omega_ref[((2 * face + b) * 5 + store) * 3 + q] * faces[2 * face + b]
                        total = term if total is None else total + term
                total = total * sign
                before = sums[component][store]
                sums[component][store] = total if before is None else before + total
    return [jnp.sum(sums[c][s], axis=0, keepdims=True) for c in range(6) for s in range(4)]


def zero_rows(n):
    return [jnp.zeros((n, 128), F32)]


def sublane_sum(tile):
    return jnp.sum(tile, axis=0, keepdims=True)


def before_image(v0_ref, local_ref, part_ref, omega_ref, pre_ref):
    share, layers = share_maps()
    norm = energy = top = bottom = jnp.zeros((8, 128), F32)
    tiles = [[v0_ref[i, 0:8, :], v0_ref[i, 8:16, :]] for i in range(8)]
    for i in range(8):
        for b in range(2):
            x = tiles[i][b]
            square = x * x * share[b]
            norm = norm + square * layers[i]
            energy = energy + x * local_ref[i, 8 * b : 8 * b + 8, :]
            if 0 < i < 7:
                bottom = bottom + square
                top = top + x * part_ref[i, 8 * b : 8 * b + 8, :] * share[b]
    rows = [sublane_sum(top), sublane_sum(norm), sublane_sum(bottom)] + zero_rows(1)
    rows += [sublane_sum(energy)] + zero_rows(3) + load_rows(face_tiles(tiles), omega_ref)
    sums = lane_sums(jnp.concatenate(rows, axis=0), 0)
    lane = lane_ids(1)
    over, norm, under, energy = sums[:, 0:1], sums[:, 1:2], sums[:, 2:3], sums[:, 4:5]
    usable = under > 1e-30
    quotient = jnp.where(usable, over / jnp.where(usable, under, 1.0), 0.0)
    quotient = jnp.clip(quotient, 0.0, 1e6)
    row = jnp.where(lane >= 8, sums, 0.0)
    for n, value in ((M, norm), (Q, energy), (S, quotient)):
        row = jnp.where(lane == n, value, row)
    pre_ref[...] = jnp.broadcast_to(row, (8, 128))


def image_sums(
    v0_ref, local_ref, part_ref, low_ref, high_ref, maps_ref, omega_ref, pre_ref, kk_ref, kr_ref,
    v1_ref, out_ref, field,
):
    share, layers = share_maps()
    low, high = in_order(low_ref[...], high_ref[...], "D")
    quotient = jnp.broadcast_to(pre_ref[:, S : S + 1], (8, 128))
    v1 = [[None] * 2 for _ in range(8)]
    u = [[None] * 2 for _ in range(8)]
    norm = cross_norm = energy = cross_energy = jnp.zeros((8, 128), F32)
    for i in range(8):
        for b in range(2):
            rows = slice(8 * b, 8 * b + 8)
            tile = part_ref[i, rows, :]
            if i == 0:
                tile = tile + low[rows, :]
            if i == 7:
                tile = tile + high[rows, :]
            v1[i][b] = tile
            v1_ref[i, rows, :] = tile
            x = v0_ref[i, rows, :]
            y = tile - quotient * x
            u[i][b] = y
            field[16 * i + 8 * b : 16 * i + 8 * b + 8, :] = y
            weighted = y * share[b] * layers[i]
            norm = norm + y * weighted
            cross_norm = cross_norm + x * weighted
            cross_energy = cross_energy + y * local_ref[i, rows, :]
    along_k = dot(field[...], kk_ref[...])
    along_j = dot(kr_ref[0:128, 0:128], field[...])
    for b in range(2):
        rows = slice(8 * b, 8 * b + 8)
        f0, f1, f2, f3 = [maps_ref[d, rows, :] for d in range(4)]
        for i in range(8):
            along_i = u[0][b] * float(STIFF[i, 0])
            for q in range(1, 8):
                along_i = along_i + u[q][b] * float(STIFF[i, q])
            at = slice(16 * i + 8 * b, 16 * i + 8 * b + 8)
            inner = f1 * along_j[at, :] + f2 * along_k[at, :] + f3 * u[i][b]
            energy = energy + u[i][b] * (f0 * along_i + float(WEIGHTS[i]) * inner)
    rows = [sublane_sum(a) for a in (norm, 2.0 * cross_norm)] + zero_rows(1)
    rows += [sublane_sum(a) for a in (energy, 2.0 * cross_energy)] + zero_rows(3)
    row = lane_sums(jnp.concatenate(rows, axis=0), 0)
    row = row + lane_sums(jnp.concatenate(load_rows(face_tiles(v1), omega_ref), axis=0), 32)
    out_ref[...] = jnp.broadcast_to(row + pre_ref[0:1, :], out_ref.shape)


def merged(parts):
    n = parts.shape[0]
    lane = lane_ids(n)
    common = parts[0:1, S : S + 1]
    e = parts[:, S : S + 1] - common
    once = jnp.where((lane == UU) | (lane == ULU), 1.0, jnp.where((lane == G2) | (lane == T2), 2.0, 0.0))
    twice = jnp.where((lane == UU) | (lane == ULU), 1.0, 0.0)
    rows = parts + e * (once * pltpu.roll(parts, 127, 1) + e * (twice * pltpu.roll(parts, 126, 1)))
    total = jnp.sum(rows, axis=0, keepdims=True)
    return jnp.where(lane_ids(1) == S, common, total)


def group_sums(parts_ref, out_ref):
    out_ref[...] = jnp.broadcast_to(merged(parts_ref[...]), out_ref.shape)


def load_column(row, first):
    place = lax.broadcasted_iota(jnp.int32, (24, 128), 0) + first
    return jnp.sum(jnp.where(lane_ids(24) == place, row, 0.0), axis=1, keepdims=True)


def finish(
    parts_ref, v0_ref, v1_ref, arm_ref, store_ref, motion_ref, p_out, velocity_out, p_ref, velocity_ref, sems
):
    total = merged(parts_ref[...])
    uu, g2, m, ulu, t2, q, s = [total[:, n : n + 1] for n in range(7)]
    alpha = m / q
    e = s - q / m
    uu = uu + e * (g2 + e * m)
    ulu = ulu + e * (t2 + e * q)
    square = alpha * alpha
    beta = square * uu / m
    curve = square * ulu - beta * beta * q
    alpha_next = square * uu / curve
    c0 = alpha + alpha_next * (1.0 + beta)
    c1 = -alpha_next * alpha
    wide0 = jnp.broadcast_to(c0, (16, 128))
    wide1 = jnp.broadcast_to(c1, (16, 128))
    for i in range(8):
        p_ref[i] = wide0 * v0_ref[i] + wide1 * v1_ref[i]
    p_copy = pltpu.make_async_copy(p_ref, p_out, sems.at[0])
    p_copy.start()
    loads = c0 * load_column(total, 8) + c1 * load_column(total, 32)
    state = motion_ref[0:24, :] + motion_ref[24:48, :] * loads
    stores = store_ref[...]
    maps = []
    for c in range(6):
        value = jnp.zeros((32, 128), F32)
        for store in range(4):
            at = 4 * c + store
            value = jnp.where(stores == store, state[at : at + 1, :], value)
        maps.append(value)
    arms = [arm_ref[c] for c in range(3)]
    for c in range(3):
        a, b = (c + 1) % 3, (c + 2) % 3
        velocity_ref[c] = maps[c] + (maps[3 + a] * arms[b] - maps[3 + b] * arms[a])
    velocity_copy = pltpu.make_async_copy(velocity_ref, velocity_out, sems.at[1])
    velocity_copy.start()
    p_copy.wait()
    velocity_copy.wait()


def spread_geometry(geo_ref, out_ref):
    element = lax.broadcasted_iota(jnp.int32, (16, 128), 0)
    out_ref[...] = dot(geo_ref[...], jnp.where((lane_ids(16) >> 3) == element, 1.0, 0.0))


def wall_table(
    elem_ref, face_ref, stores_ref, motion_ref, inverse_ref, weight_ref, arm_ref,
    table_ref, code_ref, store_out, motion_out,
):
    weight = weight_ref[...]
    nodes = jnp.concatenate([weight] + [weight * arm_ref[c] for c in range(3)], axis=0)
    a = lax.broadcasted_iota(jnp.int32, (128, 128), 0)
    b = lax.broadcasted_iota(jnp.int32, (128, 128), 1)
    slot, outer, inner = a & 64, (a >> 3) & 7, a & 7
    table_ref[0:128, :] = dot(nodes, jnp.where(b == slot + (7 - outer) * 8 + inner, 1.0, 0.0))
    table_ref[128:256, :] = dot(nodes, jnp.where(b == slot + (7 - inner) * 8 + outer, 1.0, 0.0))

    elem, face, stores = elem_ref[...], face_ref[...], stores_ref[...]
    n = lax.broadcasted_iota(jnp.int32, (1, 64), 1)
    direction = face >> 1
    first = jnp.where(direction == 2, 128, 0) + (n >> 1)
    column = elem & 15
    code_ref[0:1, :] = ((2 * face + (elem >> 4)) * 5 + stores) * 3
    code_ref[1:2, :] = column
    code_ref[2:3, :] = (8 * column + 64 * (n & 1) + 72) & 127
    code_ref[3:4, :] = first
    code_ref[4:5, :] = first + jnp.where(direction == 2, 64, 96)
    code_ref[5:6, :] = first + jnp.where(direction == 0, 64, 32)
    code_ref[6:8, :] = jnp.zeros((2, 64), jnp.int32)

    numbers = stores.astype(F32)
    row = lax.broadcasted_iota(jnp.int32, (32, 64), 0)
    column = lax.broadcasted_iota(jnp.int32, (32, 64), 1)
    even = jnp.sum(jnp.where(column == 2 * row, numbers, 0.0), axis=1, keepdims=True)
    odd = jnp.sum(jnp.where(column == 2 * row + 1, numbers, 0.0), axis=1, keepdims=True)
    store_out[...] = jnp.where(lane_ids(32) < 64, even, odd)

    load = lane_ids(8) - 8
    inside = (load >= 0) & (load < 24)
    component, store = load >> 2, load & 3
    row = row_ids()
    motion = dot(motion_ref[...], jnp.where(inside & (component == row), 1.0, 0.0)[0:6, :])
    motion = jnp.sum(jnp.where((store == row)[0:4, :], motion, 0.0), axis=0, keepdims=True)
    motion_out[0:24, :] = jnp.broadcast_to(load_column(motion, 8), (24, 128))
    scale = dot(inverse_ref[...], jnp.where(inside & (store == row), 1.0, 0.0)[0:4, :])
    taken = jnp.maximum(component - 2, 0) == row
    scale = jnp.sum(jnp.where(taken[0:4, :], scale, 0.0), axis=0, keepdims=True)
    motion_out[24:48, :] = jnp.broadcast_to(load_column(scale, 8), (24, 128))


def wall_weights(begin, end, code_ref, table_ref, *rest):
    omega_ref = rest[-1]
    if begin == 0:
        omega_ref[...] = jnp.zeros(omega_ref.shape, F32)
    lane = lane_ids() >> 3

    def add(step, carry):
        tiles = []
        for k in range(8):
            n = begin + 8 * step + k
            here = lane == code_ref[1, n]
            for q in range(3):
                nodes = jnp.broadcast_to(table_ref[pl.ds(code_ref[3 + q, n], 1), :], (8, 128))
                nodes = pltpu.roll(pltpu.roll(nodes, 0, 1, stride=8, stride_axis=0), code_ref[2, n], 1)
                tiles.append(jnp.where(here, nodes, 0.0))
        for k in range(8):
            at = code_ref[0, begin + 8 * step + k]
            for q in range(3):
                omega_ref[at + q] += tiles[3 * k + q]
        return carry

    lax.fori_loop(0, (end - begin) // 8, add, 0)


def shifted(x, axis, step, ring=False):
    count = lax.axis_size(axis)
    pairs = [(i, (i + step) % count) for i in range(count) if ring or 0 <= i + step < count]
    return lax.ppermute(x, axis, pairs)


def swapped(x, axis, first):
    pairs = [(i, i + 1) for i in range(first, lax.axis_size(axis) - 1, 2)]
    return lax.ppermute(x, axis, pairs + [(b, a) for a, b in pairs])


SWAPS = "ACD"
SPLIT = 8


STAGES = ((("vert", "span"), 32, 22), ("stream", 16, 8))


def reduced(sums):
    for at, (axes, count, first) in enumerate(STAGES):
        lists = [[(first + n) % count for n in range(count)]]
        sums = lax.all_to_all(sums.reshape(count, 1, 128), axes, 0, 0, axis_index_groups=lists).reshape(count, 128)
        if at == 0:
            sums = call(group_sums, [(STAGES[1][1], 128)])(sums)[0]
    return sums


AXIS = {"A": "stream", "B": "vert", "C": "span", "D": "stream"}
FLIPS = "D"


def swaps_at(stage):
    return int(stage in FLIPS)


def exchange(one, two, stage):
    axis = AXIS[stage]
    if stage in SWAPS:
        first = swaps_at(stage)
        return swapped(one, axis, first), swapped(two, axis, 1 - first)
    return shifted(one, axis, 1, stage == "B"), shifted(two, axis, -1, stage == "B")


def in_order(first, second, stage):
    if stage not in SWAPS:
        return first, second
    even = lax.axis_index(AXIS[stage]) % 2 == swaps_at(stage)
    return jnp.where(even, second, first), jnp.where(even, first, second)


def sent_in_order(up, down, stage):
    if stage not in SWAPS:
        return up, down
    even = lax.axis_index(AXIS[stage]) % 2 == swaps_at(stage)
    return jnp.where(even, up, down), jnp.where(even, down, up)


def per_device(
    forcing, geometry, wall_elem, wall_face, wall_store, wall_weight, wall_arm, store_motion, store_inverse
):
    lane_k, lane_i, rows, node_w = [jnp.asarray(a) for a in constants()]
    field = (8, 16, 128)
    tie = lax.optimization_barrier

    if "A" in SWAPS:
        odd = (lax.axis_index("stream") + swaps_at("A")) % 2
        top, bottom = [lax.dynamic_index_in_dim(forcing, at, 0, False) for at in (7 - 7 * odd, 7 * odd)]
    else:
        top, bottom = forcing[7], forcing[0]
    low, high = exchange(top, bottom, "A")
    geo = call(spread_geometry, [(8, 128)])(geometry.reshape(8, 16))[0]
    x, up, down = call(stream_added, [field, (72, 128), (72, 128)])(forcing, low, high, geo)

    up, down, weight, arms = tie((up, down, wall_weight.reshape(32, 128), wall_arm.reshape(3, 32, 128)))
    low, high = exchange(up, down, "B")
    table, codes, store_rows, motion = call(
        wall_table, [(256, 128), ((8, 64), jnp.int32), (32, 128), (48, 128)]
    )(wall_elem, wall_face, wall_store, store_motion.T, store_inverse, weight, arms)
    omega = call(functools.partial(wall_weights, 0, SPLIT), [(180, 8, 128)])(codes, table, smem=1)[0]
    low, high, table, codes, omega = tie((low, high, table, codes, omega))
    wide, geo_wide, right, left, to_one, to_two = call(vert_added, [(8, 32, 128), (16, 128)] + [(48, 128)] * 4)(
        x, low, high, geo
    )

    to_one, to_two, table, codes, omega = tie((to_one, to_two, table, codes, omega))
    low, high = exchange(to_one, to_two, "C")
    omega = call(functools.partial(wall_weights, SPLIT, 64), [(180, 8, 128)], input_output_aliases={2: 0})(
        codes, table, omega, smem=1
    )[0]
    low, high, omega = tie((low, high, omega))
    v0, local, part, top, bottom, maps = call(
        span_added,
        [field, field, field, (16, 128), (16, 128), (4, 16, 128)],
        scratch_shapes=[pltpu.VMEM((288, 128), F32)],
    )(wide, geo_wide, right, left, low, high, lane_k, lane_i, rows, node_w)

    low, high = exchange(top, bottom, "D")
    pre = call(before_image, [(8, 128)])(v0, local, part, omega)[0]
    v1, sums = call(image_sums, [field, (STAGES[0][1], 128)], scratch_shapes=[pltpu.VMEM((128, 128), F32)])(
        v0, local, part, low, high, maps, omega, pre, lane_k, rows
    )
    sums = reduced(sums)
    pressure, velocity = call(
        finish,
        [field, (3, 32, 128)],
        out_space=pltpu.HBM,
        scratch_shapes=[pltpu.VMEM(field, F32), pltpu.VMEM((3, 32, 128), F32), pltpu.SemaphoreType.DMA((2,))],
    )(sums, v0, v1, arms, store_rows, motion)
    return pressure, velocity.reshape(1, 3, 4096)


def solution(mesh):
    return jax.shard_map(
        per_device,
        mesh=mesh,
        in_specs=(
            P("stream", "vert", "span"),
            P(None, "stream", "vert", "span"),
            SHARDS,
            SHARDS,
            SHARDS,
            SHARDS,
            P(AXES, None, None),
            P(),
            P(),
        ),
        out_specs=(P("stream", "vert", "span"), P(AXES, None, None)),
        check_vma=False,
    )
```
